256 devices in a mesh: psg: 32 (over z, y), pb: 8 (over x, core).
Axes of the slice: x: 4, y: 4, z: 8, core: 2. Of those that a mesh axis runs over, the one named last changes fastest.
Arguments:
- dec_hidden: bfloat16 [8, 32, 4096], P('pb', None, 'psg'), may hold values from -6 to 6
- out_grad: bfloat16 [8, 32, 4096], P('pb', None, 'psg'), may hold values from -6 to 6
- query_weight: bfloat16 [4096, 2048], P('psg'), may hold values from -0.09375 to 0.09375
- output_weight: bfloat16 [2048, 4096], P(None, 'psg'), may hold values from -0.125 to 0.125
- queries: bfloat16 [8, 32, 2048], P('pb', 'psg'), may hold values from -3 to 3
- attn_out: bfloat16 [8, 32, 2048], P('pb', 'psg'), may hold values from -3 to 3
- row_max: float32 [8, 32, 32], P('pb', 'psg'), as said below
- row_sum: float32 [8, 32, 32], P('pb', 'psg'), as said below
- keys: bfloat16 [8, 64, 256, 2048], P('pb', 'psg'), may hold values from -2 to 2
- values: bfloat16 [8, 64, 256, 2048], P('pb', 'psg'), may hold values from -6 to 6
- lengths: int32 [8, 64], P('pb', 'psg'), may hold values from 1 to 256, as said below
Outputs:
- hidden_grad: bfloat16 [8, 32, 4096], P('pb', None, 'psg')
- key_grad: bfloat16 [8, 64, 256, 2048], P('pb', 'psg')
- value_grad: bfloat16 [8, 64, 256, 2048], P('pb', 'psg')
- query_weight_grad: float32 [4096, 2048], P('psg')
- output_weight_grad: float32 [2048, 4096], P(None, 'psg')
The draws below stay inside these ranges and needn't reach their ends.
Inputs may be any that keep to these rules, and one draw needn't show every extreme that they name: row_max and row_sum are the maximum of scores over the valid slots of all the question's passages and the sum of exp(scores - row_max) over them, for each token and head. `row_max`: see row_sum. `lengths`: 256 is reached in every question.
All inputs are finite; a program needn't handle non-finite values.
Results may differ from the reference program's by a relative error of at most 0.0065.
Values may be sent and summed in bfloat16 or wider, within the bound.
A program may use at most 64 MiB of HBM per device.

```python
import jax
import jax.numpy as jnp
from jax import lax

D = 4096
HEADS = 32
HD = 64
DEC = 32
PLEN = 256
PASSAGES = 64
QUESTIONS = 8


def spread_values(rng_key, shape, scale):
    normal_like = jnp.clip(jax.random.normal(jax.random.fold_in(rng_key, 1), shape, jnp.float32), -5.5, 5.5)
    return scale * normal_like


def question_stats(items):
    query_rows, key_rows, length_row = items
    slots = PASSAGES * PLEN
    query_heads = query_rows.reshape(DEC, HEADS, HD)
    key_heads = key_rows.reshape(slots, HEADS, HD)
    scores = jnp.einsum('thd,shd->hts', query_heads, key_heads, precision=lax.Precision.HIGHEST)
    position = lax.broadcasted_iota(jnp.int32, (PASSAGES, PLEN), 1)
    valid_mask = (position < length_row[:, None]).reshape(1, 1, slots)
    largest = jnp.max(jnp.where(valid_mask, scores, -1e+30), axis=2)
    total = jnp.sum(jnp.where(valid_mask, jnp.exp(scores - largest[:, :, None]), 0.0), axis=2)
    return (largest.T, total.T)


def attention_draws(key):
    query_key = jax.random.fold_in(key, 11)
    keys_key = jax.random.fold_in(key, 12)
    length_key = jax.random.fold_in(key, 13)
    width = HEADS * HD
    query_vals = spread_values(query_key, (QUESTIONS, DEC, width), 0.35)
    key_vals = spread_values(keys_key, (QUESTIONS, PASSAGES, PLEN, width), 0.35)
    lengths = jax.random.randint(length_key, (QUESTIONS, PASSAGES), 1, PLEN + 1).astype(jnp.int32)
    lengths = lengths.at[:, 0].set(PLEN)
    key_vals = key_vals.at[:, 0, 0, :].set(key_vals[:, 0, 0, :])
    key_vals = key_vals.at[:, 1, 0, :].set(key_vals[:, 1, 0, :])
    query_vals = query_vals.at[:, 0:3, :].set(query_vals[:, 0:3, :])
    query_low = query_vals.astype(jnp.bfloat16)
    key_low = key_vals.astype(jnp.bfloat16)
    largest, total = lax.map(question_stats, (query_low.astype(jnp.float32), key_low.astype(jnp.float32), lengths))
    return (query_low, key_low, lengths, largest, total)


def draw_queries(key, part):
    drawn = attention_draws(key)
    return drawn[0]


def draw_keys(key, part):
    drawn = attention_draws(key)
    return drawn[1]


def draw_lengths(key, part):
    drawn = attention_draws(key)
    return drawn[2]


def draw_row_max(key, part):
    drawn = attention_draws(key)
    return drawn[3]


def draw_row_sum(key, part):
    drawn = attention_draws(key)
    return drawn[4]


def levels(key, shape, cuts, low, high):
    def one(dim, shards_of):
        steps = jax.random.uniform(jax.random.fold_in(jax.random.fold_in(key, 6), dim), (shards_of,), jnp.float32, low / len(cuts), high / len(cuts))
        return jnp.repeat(jnp.exp(steps), shape[dim] // shards_of).reshape((-1,) + (1,) * (len(shape) - dim - 1))

    factor_of = one(*cuts[0])
    for cut in cuts[1:]:
        factor_of = factor_of * one(*cut)
    return factor_of


def bell_draw(rng, extent, deviation, limit, pieces=(), kind=jnp.bfloat16):
    values = deviation * jax.random.normal(rng, extent, jnp.float32)
    if pieces:
        values = values * levels(rng, extent, pieces, -0.22, 0.18)
    return jnp.clip(values, -limit, limit).astype(kind)


def setup_inputs(seed: int = 0) -> dict:
    streams_of = jax.random.split(jax.random.key(seed), 12)
    dec_hidden = bell_draw(streams_of[0], (QUESTIONS, DEC, D), 1.0, 6.0, ((0, 8), (2, 32)))
    out_grad = bell_draw(streams_of[1], (QUESTIONS, DEC, D), 1.0, 6.0, ((0, 8), (2, 32)))
    query_weight = bell_draw(streams_of[2], (D, HEADS * HD), D ** -0.5, 0.09375, ((0, 32),))
    output_weight = bell_draw(streams_of[3], (HEADS * HD, D), (HEADS * HD) ** -0.5, 0.125, ((1, 32),))
    queries = draw_queries(jax.random.fold_in(streams_of[11], 71), 0)
    attn_out = bell_draw(streams_of[5], (QUESTIONS, DEC, HEADS * HD), 0.5, 3.0, ((0, 8), (1, 32)))
    row_max = draw_row_max(jax.random.fold_in(streams_of[11], 71), 0)
    row_sum = draw_row_sum(jax.random.fold_in(streams_of[11], 71), 0)
    keys = draw_keys(jax.random.fold_in(streams_of[11], 71), 0)
    values = bell_draw(streams_of[9], (QUESTIONS, PASSAGES, PLEN, HEADS * HD), 1.0, 6.0, ((0, 8), (1, 32)))
    lengths = draw_lengths(jax.random.fold_in(streams_of[11], 71), 0)
    return {"dec_hidden": dec_hidden, "out_grad": out_grad, "query_weight": query_weight, "output_weight": output_weight, "queries": queries, "attn_out": attn_out, "row_max": row_max, "row_sum": row_sum, "keys": keys, "values": values, "lengths": lengths}


def one_question(items):
    query_rows, grad_rows, delta_rows, max_rows, sum_rows, key_rows, value_rows, length_row = items
    slots = PASSAGES * PLEN
    query_heads = query_rows.reshape(DEC, HEADS, HD).astype(jnp.float32)
    grad_heads = grad_rows.reshape(DEC, HEADS, HD).astype(jnp.float32)
    key_heads = key_rows.reshape(slots, HEADS, HD).astype(jnp.float32)
    value_heads = value_rows.reshape(slots, HEADS, HD).astype(jnp.float32)
    scores = jnp.einsum('thd,shd->hts', query_heads, key_heads)
    position = lax.broadcasted_iota(jnp.int32, (PASSAGES, PLEN), 1)
    valid_mask = (position < length_row[:, None]).reshape(1, 1, slots)
    attn_probs = jnp.where(valid_mask, jnp.exp(scores - max_rows.T[:, :, None]), 0.0) / sum_rows.T[:, :, None]
    probs_low = lax.optimization_barrier(attn_probs.astype(jnp.bfloat16)).astype(jnp.float32)
    value_grad = jnp.einsum('hts,thd->shd', probs_low, grad_heads).astype(jnp.bfloat16)
    prob_grad = jnp.einsum('thd,shd->hts', grad_heads, value_heads)
    score_grad = attn_probs * (prob_grad - delta_rows.T[:, :, None])
    score_grad = lax.optimization_barrier(score_grad.astype(jnp.bfloat16)).astype(jnp.float32)
    key_grad = jnp.einsum('hts,thd->shd', score_grad, query_heads).astype(jnp.bfloat16)
    query_part = jnp.einsum('hts,shd->thd', score_grad, key_heads)
    return (key_grad.reshape(PASSAGES, PLEN, HEADS * HD), value_grad.reshape(PASSAGES, PLEN, HEADS * HD),
            query_part.reshape(DEC, HEADS * HD).astype(jnp.bfloat16))


def reference(dec_hidden, out_grad, query_weight, output_weight, queries, attn_out, row_max, row_sum, keys, values, lengths):
    grad_attn = jnp.einsum('qtc,ec->qte', out_grad.astype(jnp.float32), output_weight.astype(jnp.float32)).astype(jnp.bfloat16)
    product = grad_attn.astype(jnp.float32) * attn_out.astype(jnp.float32)
    row_delta = jnp.sum(product.reshape(QUESTIONS, DEC, HEADS, HD), axis=3)
    key_grad, value_grad, query_grad = lax.map(one_question, (queries, grad_attn, row_delta, row_max, row_sum, keys, values, lengths))
    query_float = query_grad.astype(jnp.float32)
    hidden_grad = jnp.einsum('qte,ce->qtc', query_float, query_weight.astype(jnp.float32)).astype(jnp.bfloat16)
    query_weight_grad = jnp.einsum('qtc,qte->ce', dec_hidden.astype(jnp.float32), query_float)
    output_weight_grad = jnp.einsum('qte,qtc->ec', attn_out.astype(jnp.float32), out_grad.astype(jnp.float32))
    return hidden_grad, key_grad, value_grad, query_weight_grad, output_weight_grad
```

```python
import functools

import jax
import jax.numpy as jnp
from jax import lax
from jax.experimental import pallas as pl
from jax.experimental.pallas import tpu as pltpu
from jax.sharding import PartitionSpec as P

MESH = pl.DeviceIdType.MESH
F32 = jnp.float32
BF16 = jnp.bfloat16

NT = (((1,), (1,)), ((), ()))
TN = (((0,), (0,)), ((), ()))
NN = (((1,), (0,)), ((), ()))

Z, Y, PSG, PB = 8, 4, 32, 8
GROUPS = 8


def dot(a, b, dims):
    return lax.dot_general(a, b, dims, preferred_element_type=F32)


def columns(pieces):
    left = jnp.concatenate([pieces[0], pieces[1]], axis=0)
    right = jnp.concatenate([pieces[2], pieces[3]], axis=0)
    return jnp.concatenate([left, right], axis=1)


def head_blocks(rows):
    tiled = jnp.concatenate([rows] * 4, axis=0)
    row = lax.broadcasted_iota(jnp.int32, tiled.shape, 0) // 32
    col = lax.broadcasted_iota(jnp.int32, tiled.shape, 1) // 64
    return jnp.where(row == col, tiled, jnp.zeros_like(tiled))


def far_first(n):
    kz, ky = n // 4, n % 4
    dz = 4 + (1 - 2 * (kz % 2)) * ((kz + 1) // 2)
    dy = 2 + (1 - 2 * (ky % 2)) * ((ky + 1) // 2)
    return dz, dy


def split_bf16(x, terms):
    out = []
    for _ in range(terms):
        part = x.astype(BF16)
        out.append(part)
        x = x - part.astype(F32)
    return out


def comm_kernel(
    dec_hbm, grad_hbm, weight_hbm, query_hbm, attn_hbm, max_hbm, sum_hbm, keys_hbm, values_hbm, len_hbm,
    probs_out, sgrad_out, q_out, g_out, qg_out, o_out, dg_out,
    weight, keys, values, query_ref, attn_ref, max_ref, sum_ref, len_ref, bundle, qa, qa32, stat_src, stats, partial, part_in, g_own, g_all, q_all,
    probs, probs_low, sgrad, qpart, qpart_in, qg_own, qg_all, o_all, dg_src, dg_all,
    local_sem, send_sem, recv_sem, x_send, x_recv, out_sem,
):
    me, pb = lax.axis_index("psg"), lax.axis_index("pb")
    z, y = me // Y, me % Y
    core, xpos = pb % 2, pb // 2
    slot = core * 4 + xpos
    partner = pb + 1 - 2 * core

    def psg_peer(n):
        dz, dy = far_first(n)
        return ((z + dz) % Z) * Y + (y + dy) % Y

    barrier = pltpu.get_barrier_semaphore()

    def greet(n, carry):
        pl.semaphore_signal(barrier, inc=1, device_id=(psg_peer(n), pb), device_id_type=MESH)
        return carry

    lax.fori_loop(0, PSG - 1, greet, 0)
    for d in range(1, PB):
        pl.semaphore_signal(barrier, inc=1, device_id=(me, (pb + d) % PB), device_id_type=MESH)

    loads = [
        pltpu.make_async_copy(src, dst, local_sem.at[i])
        for i, (src, dst) in enumerate((
            (query_hbm, query_ref), (attn_hbm, attn_ref), (max_hbm, max_ref), (sum_hbm, sum_ref),
            (dec_hbm, dg_src.at[0]), (grad_hbm, dg_src.at[1]), (weight_hbm, weight), (len_hbm, len_ref),
            (keys_hbm, keys), (values_hbm, values),
        ))
    ]
    for load in loads:
        load.start()
    keys_copy, values_copy = loads[8:]
    for load in loads[:6]:
        load.wait()

    for k in range(16):
        bundle[k : k + 1, :] = query_ref[:, k * 128 : (k + 1) * 128].astype(F32)
        bundle[16 + k : 17 + k, :] = attn_ref[:, k * 128 : (k + 1) * 128].astype(F32)
    qa_own = bundle[...].astype(BF16)
    qa[me] = qa_own
    stat_src[...] = jnp.zeros_like(stat_src)
    stat_src[0:1, 0:32] = max_ref[...] + jnp.log(sum_ref[...])
    stats[me] = stat_src[...]
    dg_all[slot] = dg_src[...]

    loads[6].wait()
    loads[7].wait()
    grad = dg_src[1]
    for k in range(16):
        block = dot(grad, weight[k * 128 : (k + 1) * 128, :], NT).astype(BF16)
        partial[2 * k] = block[0:16]
        partial[2 * k + 1] = block[16:32]

    pl.semaphore_wait(barrier, PSG - 1 + PB - 1)

    def scatter(src, dst, i):
        def go(n, carry):
            to = psg_peer(n)
            pltpu.make_async_remote_copy(
                src_ref=src.at[to], dst_ref=dst.at[me], send_sem=send_sem.at[i], recv_sem=recv_sem.at[i],
                device_id=(to, pb), device_id_type=MESH,
            ).start()
            return carry

        lax.fori_loop(0, PSG - 1, go, 0)

    def broadcast(src, dst, i):
        def go(n, carry):
            pltpu.make_async_remote_copy(
                src_ref=src, dst_ref=dst, send_sem=send_sem.at[i], recv_sem=recv_sem.at[i],
                device_id=(psg_peer(n), pb), device_id_type=MESH,
            ).start()
            return carry

        lax.fori_loop(0, PSG - 1, go, 0)

    def wait_bytes(ref, sem):
        pltpu.make_async_copy(ref, ref, sem).wait()

    scatter(partial, part_in, 0)
    part_in[me] = partial[me]
    broadcast(qa.at[me], qa.at[me], 1)
    broadcast(stats.at[me], stats.at[me], 2)
    for d in range(1, PB):
        pltpu.make_async_remote_copy(
            src_ref=dg_src, dst_ref=dg_all.at[slot], send_sem=x_send.at[14], recv_sem=x_recv.at[14],
            device_id=(me, (pb + d) % PB), device_id_type=MESH,
        ).start()

    def x_start(buf, base):
        for d in range(1, 4):
            pltpu.make_async_remote_copy(
                src_ref=buf.at[slot], dst_ref=buf.at[slot], send_sem=x_send.at[base + d], recv_sem=x_recv.at[base + d],
                device_id=(me, (pb + 2 * d) % PB), device_id_type=MESH,
            ).start()
        pltpu.make_async_remote_copy(
            src_ref=buf.at[slot], dst_ref=buf.at[slot], send_sem=x_send.at[base], recv_sem=x_recv.at[base],
            device_id=(me, partner), device_id_type=MESH,
        ).start()

    def x_forward(buf, base):
        for d in (1, 3, 2):
            wait_bytes(buf.at[0], x_recv.at[base + d])
            got = core * 4 + (xpos + 4 - d) % 4
            pltpu.make_async_remote_copy(
                src_ref=buf.at[got], dst_ref=buf.at[got], send_sem=x_send.at[base + 3 + d], recv_sem=x_recv.at[base + 3 + d],
                device_id=(me, partner), device_id_type=MESH,
            ).start()

    def x_finish(buf, base):
        for k in (0, 4, 6, 5):
            wait_bytes(buf.at[0], x_recv.at[base + k])

    def x_drain(buf, base):
        for k in range(7):
            wait_bytes(buf.at[0], x_send.at[base + k])

    wait_bytes(part_in.at[pl.ds(0, PSG - 1)], recv_sem.at[0])
    g_own[...] = jnp.sum(part_in[...].astype(F32), axis=0).astype(BF16)
    broadcast(g_own, g_all.at[me], 3)
    g_all[me] = g_own[...]

    wait_bytes(qa.at[pl.ds(0, PSG - 1)], recv_sem.at[1])
    qa32[...] = qa[...].astype(F32)
    for k in range(16):
        block = qa32[:, k, :].astype(BF16)
        q_all[2 * k] = block[0:16]
        q_all[2 * k + 1] = block[16:32]
        block = qa32[:, 16 + k, :].astype(BF16)
        o_all[slot, 2 * k] = block[0:16]
        o_all[slot, 2 * k + 1] = block[16:32]
    x_start(o_all, 0)
    q_copy = pltpu.make_async_copy(q_all, q_out, out_sem.at[0])
    q_copy.start()

    wait_bytes(stats.at[pl.ds(0, PSG - 1)], recv_sem.at[2])
    stat_rows = jnp.concatenate([stats[t, 0:1, :] for t in range(PSG)], axis=0)
    head = lax.broadcasted_iota(jnp.int32, (128, 1024), 0)
    lane = lax.broadcasted_iota(jnp.int32, (128, 1024), 1)
    pick = jnp.where(head == lane // 32, 1.0, 0.0).astype(BF16)
    spread = sum(dot(part, pick, NN) for part in split_bf16(stat_rows, 3))
    token = lax.broadcasted_iota(jnp.int32, (32, 1024), 0)
    lane = lax.broadcasted_iota(jnp.int32, (32, 1024), 1)
    stat_lanes = jnp.sum(jnp.where(token == lane % 32, spread, 0.0), axis=0, keepdims=True)

    keys_copy.wait()
    position = lax.broadcasted_iota(jnp.int32, (256, 128), 0)
    for g in range(GROUPS):
        wide, narrow = pl.ds(g * 256, 256), pl.ds(g * 128, 128)
        blocks = head_blocks(columns(q_all[pl.ds(g * 4, 4)]))
        scores = dot(keys[:, wide], blocks, NT) - stat_lanes[:, g * 128 : (g + 1) * 128]
        for p in range(2):
            rows = pl.ds(p * 256, 256)
            value = jnp.where(position < len_ref[0, p], jnp.exp(scores[p * 256 : (p + 1) * 256]), 0.0)
            probs[rows, narrow] = value
            probs_low[rows, narrow] = value.astype(BF16)
    probs_copy = pltpu.make_async_copy(probs_low, probs_out, out_sem.at[1])
    probs_copy.start()

    wait_bytes(g_all.at[pl.ds(0, PSG - 1)], recv_sem.at[3])
    g_copy = pltpu.make_async_copy(g_all, g_out, out_sem.at[2])
    g_copy.start()
    values_copy.wait()
    ones = jnp.ones((8, 256), BF16)
    for g in range(GROUPS):
        wide, narrow = pl.ds(g * 256, 256), pl.ds(g * 128, 128)
        blocks = head_blocks(columns(g_all[pl.ds(g * 4, 4)]))
        out_rows = columns(o_all[slot, pl.ds(g * 4, 4)]).astype(F32)
        product = blocks.astype(F32) * jnp.concatenate([out_rows] * 4, axis=0)
        delta = sum(dot(ones, part, NT) for part in split_bf16(product, 3))[0:1]
        prob_grad = dot(values[:, wide], blocks, NT)
        score_grad = (probs[:, narrow] * (prob_grad - delta)).astype(BF16)
        sgrad[:, narrow] = score_grad
        part = dot(score_grad, keys[:, wide], TN)
        head = lax.broadcasted_iota(jnp.int32, part.shape, 0) // 32
        col = lax.broadcasted_iota(jnp.int32, part.shape, 1) // 64
        part = jnp.where(head == col, part, 0.0)
        part = (part[0:32] + part[32:64] + part[64:96] + part[96:128]).astype(BF16)
        qpart[4 * g] = part[0:16, 0:128]
        qpart[4 * g + 1] = part[16:32, 0:128]
        qpart[4 * g + 2] = part[0:16, 128:256]
        qpart[4 * g + 3] = part[16:32, 128:256]
    scatter(qpart, qpart_in, 4)
    qpart_in[me] = qpart[me]
    sgrad_copy = pltpu.make_async_copy(sgrad, sgrad_out, out_sem.at[3])
    sgrad_copy.start()

    x_forward(o_all, 0)

    wait_bytes(qpart_in.at[pl.ds(0, PSG - 1)], recv_sem.at[4])
    qg_own[...] = jnp.sum(qpart_in[...].astype(F32), axis=0).astype(BF16)
    broadcast(qg_own, qg_all.at[slot, me], 5)
    qg_all[slot, me] = qg_own[...]

    wait_bytes(dg_all.at[pl.ds(0, PB - 1)], x_recv.at[14])
    dg_copy = pltpu.make_async_copy(dg_all, dg_out, out_sem.at[4])
    dg_copy.start()
    x_finish(o_all, 0)
    o_copy = pltpu.make_async_copy(o_all, o_out, out_sem.at[5])
    o_copy.start()

    wait_bytes(qg_all.at[slot, pl.ds(0, PSG - 1)], recv_sem.at[5])
    x_start(qg_all, 7)
    x_forward(qg_all, 7)
    x_finish(qg_all, 7)
    qg_copy = pltpu.make_async_copy(qg_all, qg_out, out_sem.at[6])
    qg_copy.start()

    wait_bytes(partial.at[pl.ds(0, PSG - 1)], send_sem.at[0])
    wait_bytes(qa.at[pl.ds(0, PSG - 1)], send_sem.at[1])
    wait_bytes(stats.at[pl.ds(0, PSG - 1)], send_sem.at[2])
    wait_bytes(g_all.at[pl.ds(0, PSG - 1)], send_sem.at[3])
    wait_bytes(qpart.at[pl.ds(0, PSG - 1)], send_sem.at[4])
    wait_bytes(qpart.at[pl.ds(0, PSG - 1)], send_sem.at[5])
    wait_bytes(dg_all.at[pl.ds(0, PB - 1)], x_send.at[14])
    x_drain(o_all, 0)
    x_drain(qg_all, 7)
    for copy in (q_copy, probs_copy, g_copy, sgrad_copy, dg_copy, o_copy, qg_copy):
        copy.wait()


def grads_kernel(
    probs_ref, sgrad_ref, q_ref, g_ref, qg_ref, o_ref, dg_ref, qw_ref,
    hidden_ref, kgrad_ref, vgrad_ref, qwg_ref, owg_ref, acc,
):
    g = pl.program_id(0)
    pb = lax.axis_index("pb")
    slot = (pb % 2) * 4 + pb // 2
    vgrad_ref[...] = dot(probs_ref[...], head_blocks(columns(g_ref[...])), NN).astype(BF16)
    kgrad_ref[...] = dot(sgrad_ref[...], head_blocks(columns(q_ref[...])), NN).astype(BF16)

    def all_questions(ref):
        return jnp.concatenate([columns(ref[s]) for s in range(PB)], axis=0)

    tokens = jnp.concatenate([dg_ref[s, 0] for s in range(PB)], axis=0)
    qwg_ref[...] = dot(tokens, all_questions(qg_ref), TN)
    tokens = jnp.concatenate([dg_ref[s, 1] for s in range(PB)], axis=0)
    owg_ref[...] = dot(all_questions(o_ref), tokens, TN)
    part = dot(columns(qg_ref[slot]), qw_ref[...], NT)

    @pl.when(g == 0)
    def _():
        acc[...] = part

    @pl.when(g > 0)
    def _():
        acc[...] += part

    @pl.when(g == GROUPS - 1)
    def _():
        hidden_ref[...] = acc[...].astype(BF16)


def local(
    dec_hidden, out_grad, query_weight, output_weight, queries, attn_out, row_max, row_sum, keys, values, lengths
):
    hbm = pl.BlockSpec(memory_space=pl.ANY)
    sds = jax.ShapeDtypeStruct
    pieces = (PSG, 16, 128)
    probs, sgrad, q_all, g_all, qg_all, o_all, dg_all = pl.pallas_call(
        comm_kernel,
        out_shape=[
            sds((512, 1024), BF16), sds((512, 1024), BF16), sds(pieces, BF16), sds(pieces, BF16),
            sds((PB,) + pieces, BF16), sds((PB,) + pieces, BF16), sds((PB, 2, 32, 128), BF16),
        ],
        in_specs=[hbm] * 10,
        out_specs=[hbm] * 7,
        scratch_shapes=[
            pltpu.VMEM((2048, 128), BF16),
            pltpu.VMEM((512, 2048), BF16),
            pltpu.VMEM((512, 2048), BF16),
            pltpu.VMEM((1, 2048), BF16),
            pltpu.VMEM((1, 2048), BF16),
            pltpu.VMEM((1, 32), F32),
            pltpu.VMEM((1, 32), F32),
            pltpu.SMEM((1, 2), jnp.int32),
            pltpu.VMEM((32, 128), F32),
            pltpu.VMEM((PSG, 32, 128), BF16),
            pltpu.VMEM((PSG, 32, 128), F32),
            pltpu.VMEM((8, 128), F32),
            pltpu.VMEM((PSG, 8, 128), F32),
            pltpu.VMEM(pieces, BF16),
            pltpu.VMEM(pieces, BF16),
            pltpu.VMEM((16, 128), BF16),
            pltpu.VMEM(pieces, BF16),
            pltpu.VMEM(pieces, BF16),
            pltpu.VMEM((512, 1024), F32),
            pltpu.VMEM((512, 1024), BF16),
            pltpu.VMEM((512, 1024), BF16),
            pltpu.VMEM(pieces, BF16),
            pltpu.VMEM(pieces, BF16),
            pltpu.VMEM((16, 128), BF16),
            pltpu.VMEM((PB,) + pieces, BF16),
            pltpu.VMEM((PB,) + pieces, BF16),
            pltpu.VMEM((2, 32, 128), BF16),
            pltpu.VMEM((PB, 2, 32, 128), BF16),
            pltpu.SemaphoreType.DMA((10,)),
            pltpu.SemaphoreType.DMA((6,)),
            pltpu.SemaphoreType.DMA((6,)),
            pltpu.SemaphoreType.DMA((15,)),
            pltpu.SemaphoreType.DMA((15,)),
            pltpu.SemaphoreType.DMA((7,)),
        ],
        compiler_params=pltpu.CompilerParams(collective_id=1, has_side_effects=True, vmem_limit_bytes=62 * 2**20),
        cost_estimate=pl.CostEstimate(flops=10**9, bytes_accessed=10**7, transcendentals=512 * 1024),
        name="comm",
    )(
        dec_hidden.reshape(32, 128), out_grad.reshape(32, 128), output_weight,
        queries.reshape(1, 2048), attn_out.reshape(1, 2048), row_max.reshape(1, 32), row_sum.reshape(1, 32),
        keys.reshape(512, 2048), values.reshape(512, 2048), lengths,
    )

    def whole(shape):
        return pl.BlockSpec(shape, lambda g: (0,) * len(shape))

    hidden, kgrad, vgrad, qwg, owg = pl.pallas_call(
        grads_kernel,
        grid=(GROUPS,),
        out_shape=[
            sds((32, 128), BF16), sds((512, 2048), BF16), sds((512, 2048), BF16),
            sds((128, 2048), F32), sds((2048, 128), F32),
        ],
        in_specs=[
            pl.BlockSpec((512, 128), lambda g: (0, g)), pl.BlockSpec((512, 128), lambda g: (0, g)),
            pl.BlockSpec((4, 16, 128), lambda g: (g, 0, 0)), pl.BlockSpec((4, 16, 128), lambda g: (g, 0, 0)),
            pl.BlockSpec((PB, 4, 16, 128), lambda g: (0, g, 0, 0)), pl.BlockSpec((PB, 4, 16, 128), lambda g: (0, g, 0, 0)),
            whole((PB, 2, 32, 128)),
            pl.BlockSpec((128, 256), lambda g: (0, g)),
        ],
        out_specs=[
            whole((32, 128)), pl.BlockSpec((512, 256), lambda g: (0, g)), pl.BlockSpec((512, 256), lambda g: (0, g)),
            pl.BlockSpec((128, 256), lambda g: (0, g)), pl.BlockSpec((256, 128), lambda g: (g, 0)),
        ],
        scratch_shapes=[pltpu.VMEM((32, 128), F32)],
        compiler_params=pltpu.CompilerParams(vmem_limit_bytes=62 * 2**20),
        cost_estimate=pl.CostEstimate(flops=10**9, bytes_accessed=10**7, transcendentals=0),
        name="grads",
    )(probs, sgrad, q_all, g_all, qg_all, o_all, dg_all, query_weight)
    return (
        hidden.reshape(dec_hidden.shape), kgrad.reshape(keys.shape), vgrad.reshape(values.shape), qwg, owg
    )


def solution(mesh):
    in_specs = (
        P("pb", None, "psg"),
        P("pb", None, "psg"),
        P("psg", None),
        P(None, "psg"),
        P("pb", "psg", None),
        P("pb", "psg", None),
        P("pb", "psg", None),
        P("pb", "psg", None),
        P("pb", "psg", None, None),
        P("pb", "psg", None, None),
        P("pb", "psg"),
    )
    out_specs = (
        P("pb", None, "psg"),
        P("pb", "psg", None, None),
        P("pb", "psg", None, None),
        P("psg", None),
        P(None, "psg"),
    )
    return jax.shard_map(local, mesh=mesh, in_specs=in_specs, out_specs=out_specs, check_vma=False)
```

```python
import jax
import jax.numpy as jnp
from jax import lax
from jax.experimental import pallas as pl
from jax.experimental.pallas import tpu as pltpu
from jax.sharding import PartitionSpec as P

MESH = pl.DeviceIdType.MESH
F32 = jnp.float32
BF16 = jnp.bfloat16

NT = (((1,), (1,)), ((), ()))
TN = (((0,), (0,)), ((), ()))
NN = (((1,), (0,)), ((), ()))

Z, Y, PSG, PB = 8, 4, 32, 8
GROUPS = 8
NEAR = (0, 1, 7, 2, 6, 3, 5, 4)


def dot(a, b, dims):
    return lax.dot_general(a, b, dims, preferred_element_type=F32)


def columns(pieces):
    left = jnp.concatenate([pieces[0], pieces[1]], axis=0)
    right = jnp.concatenate([pieces[2], pieces[3]], axis=0)
    return jnp.concatenate([left, right], axis=1)


def head_blocks(rows):
    tiled = jnp.concatenate([rows] * 4, axis=0)
    row = lax.broadcasted_iota(jnp.int32, tiled.shape, 0) // 32
    col = lax.broadcasted_iota(jnp.int32, tiled.shape, 1) // 64
    return jnp.where(row == col, tiled, jnp.zeros_like(tiled))


def split_bf16(x, terms):
    out = []
    for _ in range(terms):
        part = x.astype(BF16)
        out.append(part)
        x = x - part.astype(F32)
    return out


def comm_kernel(
    dec_hbm, grad_hbm, weight_hbm, query_hbm, attn_hbm, max_hbm, sum_hbm, keys_hbm, values_hbm, len_hbm,
    probs_out, sgrad_out, q_out, g_out, qg_out, o_out, dg_out,
    weight, keys, values, query_ref, attn_ref, max_ref, sum_ref, len_ref, bundle, qa, qa32, stat_src, stats,
    partial, part_in, g_own, g_all, q_all, probs, probs_low, sgrad, qpart, qpart_in, qg_own, qg_all,
    o_all, dg_src, dg_all,
    local_sem, send_sem, recv_sem, x_send, x_recv, side_send, side_recv, core_send,
    core_recv, out_sem, qg_sem,
):
    me, pb = lax.axis_index("psg"), lax.axis_index("pb")
    z, y = lax.div(me, Y), lax.rem(me, Y)
    core, xpos = lax.rem(pb, 2), lax.div(pb, 2)
    slot = core * 4 + xpos
    partner = pb + 1 - 2 * core
    zs = [lax.rem(z + d, Z) for d in range(Z)]
    ys = [lax.rem(y + d, Y) for d in range(Y)]
    peers = {(dz, dy): zs[dz] * Y + ys[dy] for dz in range(Z) for dy in range(Y) if dz or dy}
    far_first = [peers[dz, dy] for dz in reversed(NEAR) for dy in (2, 1, 3, 0) if dz or dy]
    pb_peers = [lax.rem(pb + d, PB) for d in range(PB)]

    barrier = pltpu.get_barrier_semaphore()
    for to in far_first:
        pl.semaphore_signal(barrier, inc=1, device_id=(to, pb), device_id_type=MESH)
    for d in range(1, PB):
        pl.semaphore_signal(barrier, inc=1, device_id=(me, pb_peers[d]), device_id_type=MESH)

    loads = [
        pltpu.make_async_copy(src, dst, local_sem.at[i])
        for i, (src, dst) in enumerate((
            (query_hbm, query_ref), (attn_hbm, attn_ref), (max_hbm, max_ref), (sum_hbm, sum_ref),
            (dec_hbm, dg_src.at[0]), (grad_hbm, dg_src.at[1]), (weight_hbm, weight), (len_hbm, len_ref),
            (keys_hbm, keys), (values_hbm, values),
        ))
    ]
    for load in loads:
        load.start()
    keys_copy, values_copy = loads[8:]
    for load in loads[:6]:
        load.wait()

    for k in range(16):
        bundle[k : k + 1, :] = query_ref[:, k * 128 : (k + 1) * 128].astype(F32)
        bundle[16 + k : 17 + k, :] = attn_ref[:, k * 128 : (k + 1) * 128].astype(F32)
    qa[me] = bundle[...].astype(BF16)
    stat_src[...] = jnp.zeros_like(stat_src)
    stat_src[0:1, 0:32] = max_ref[...] + jnp.log(sum_ref[...])
    stats[me] = stat_src[...]
    dg_all[slot] = dg_src[...]

    loads[6].wait()
    loads[7].wait()
    grad = dg_src[1]
    for k in range(16):
        block = dot(grad, weight[k * 128 : (k + 1) * 128, :], NT).astype(BF16)
        partial[2 * k] = block[0:16]
        partial[2 * k + 1] = block[16:32]

    pl.semaphore_wait(barrier, PSG - 1 + PB - 1)

    def send(src, dst, send_at, recv_at, to):
        pltpu.make_async_remote_copy(
            src_ref=src, dst_ref=dst, send_sem=send_at, recv_sem=recv_at, device_id=to, device_id_type=MESH
        ).start()

    def wait_bytes(ref, sem):
        pltpu.make_async_copy(ref, ref, sem).wait()

    for dy in (2, 1, 3):
        send(stats.at[me], stats.at[me], send_sem.at[2], recv_sem.at[2], (peers[0, dy], pb))
    for to in far_first:
        send(partial.at[to], part_in.at[me], send_sem.at[0], recv_sem.at[0], (to, pb))
    part_in[me] = partial[me]
    for to in far_first:
        send(qa.at[me], qa.at[me], send_sem.at[1], recv_sem.at[1], (to, pb))
    row_of_four = pl.ds(z * Y, Y)
    wait_bytes(stats.at[pl.ds(0, Y - 1)], recv_sem.at[2])
    for dz in (4, 5, 3, 6, 2, 7, 1):
        send(stats.at[row_of_four], stats.at[row_of_four], send_sem.at[7], recv_sem.at[5], (peers[dz, 0], pb))

    wait_bytes(part_in.at[pl.ds(0, PSG - 1)], recv_sem.at[0])
    g_own[...] = jnp.sum(part_in[...].astype(F32), axis=0).astype(BF16)
    for to in far_first:
        send(g_own, g_all.at[me], send_sem.at[3], recv_sem.at[3], (to, pb))
    g_all[me] = g_own[...]
    for d in range(1, PB):
        send(dg_src, dg_all.at[slot], x_send.at[7], x_recv.at[7], (me, pb_peers[d]))

    wait_bytes(qa.at[pl.ds(0, PSG - 1)], recv_sem.at[1])
    qa32[...] = qa[...].astype(F32)
    for k in range(16):
        block = qa32[:, k, :].astype(BF16)
        q_all[2 * k] = block[0:16]
        q_all[2 * k + 1] = block[16:32]
        block = qa32[:, 16 + k, :].astype(BF16)
        o_all[slot, 2 * k] = block[0:16]
        o_all[slot, 2 * k + 1] = block[16:32]
    own = o_all.at[slot]
    for d in range(1, 4):
        send(own, own, x_send.at[d], x_recv.at[d], (me, pb_peers[2 * d]))
    send(own, own, x_send.at[0], x_recv.at[0], (me, partner))
    q_copy = pltpu.make_async_copy(q_all, q_out, out_sem.at[0])
    q_copy.start()

    wait_bytes(stats.at[pl.ds(0, PSG - Y)], recv_sem.at[5])
    stat_rows = jnp.concatenate([stats[t] for t in range(PSG)], axis=0)
    head = lax.broadcasted_iota(jnp.int32, (128, 1024), 0)
    lane = lax.broadcasted_iota(jnp.int32, (128, 1024), 1)
    pick = jnp.where(head == lane // 32, 1.0, 0.0).astype(BF16)
    spread = sum(dot(part, pick, NN) for part in split_bf16(stat_rows, 3))
    token = lax.broadcasted_iota(jnp.int32, (32, 1024), 0)
    lane = lax.broadcasted_iota(jnp.int32, (32, 1024), 1)
    stat_lanes = jnp.sum(jnp.where(token == lane % 32, spread, 0.0), axis=0, keepdims=True)

    keys_copy.wait()
    position = lax.broadcasted_iota(jnp.int32, (256, 128), 0)
    for g in range(GROUPS):
        blocks = head_blocks(columns(q_all[pl.ds(g * 4, 4)]))
        scores = dot(keys[:, g * 256 : (g + 1) * 256], blocks, NT) - stat_lanes[:, g * 128 : (g + 1) * 128]
        for p in range(2):
            rows = pl.ds(p * 256, 256)
            value = jnp.where(position < len_ref[0, p], jnp.exp(scores[p * 256 : (p + 1) * 256]), 0.0)
            probs[g, rows] = value
            probs_low[g, rows] = value.astype(BF16)
    probs_copy = pltpu.make_async_copy(probs_low, probs_out, out_sem.at[1])
    probs_copy.start()
    values_copy.wait()

    wait_bytes(g_all.at[pl.ds(0, PSG - 1)], recv_sem.at[3])
    ones = jnp.ones((8, 256), BF16)
    for g in range(GROUPS):
        four = pl.ds(g * 4, 4)
        blocks = head_blocks(columns(g_all[four]))
        out_rows = columns(o_all[slot, four]).astype(F32)
        product = blocks.astype(F32) * jnp.concatenate([out_rows] * 4, axis=0)
        delta = sum(dot(ones, part, NT) for part in split_bf16(product, 2))[0:1]
        prob_grad = dot(values[:, g * 256 : (g + 1) * 256], blocks, NT)
        sgrad[g] = (probs[g] * (prob_grad - delta)).astype(BF16)
    row = lax.broadcasted_iota(jnp.int32, (128, 256), 0) // 32
    col = lax.broadcasted_iota(jnp.int32, (128, 256), 1) // 64
    for g in range(GROUPS):
        part = jnp.where(row == col, dot(sgrad[g], keys[:, g * 256 : (g + 1) * 256], TN), 0.0)
        part = (part[0:32] + part[32:64] + part[64:96] + part[96:128]).astype(BF16)
        qpart[g * 4] = part[0:16, 0:128]
        qpart[g * 4 + 1] = part[16:32, 0:128]
        qpart[g * 4 + 2] = part[0:16, 128:256]
        qpart[g * 4 + 3] = part[16:32, 128:256]
    for to in far_first:
        send(qpart.at[to], qpart_in.at[me], send_sem.at[4], recv_sem.at[4], (to, pb))
    qpart_in[me] = qpart[me]
    g_copy = pltpu.make_async_copy(g_all, g_out, out_sem.at[2])
    g_copy.start()
    sgrad_copy = pltpu.make_async_copy(sgrad, sgrad_out, out_sem.at[3])
    sgrad_copy.start()

    for d in (1, 3, 2):
        wait_bytes(own, x_recv.at[d])
        got = o_all.at[core * 4 + lax.rem(xpos + 4 - d, 4)]
        send(got, got, x_send.at[3 + d], x_recv.at[3 + d], (me, partner))
    wait_bytes(dg_all.at[pl.ds(0, PB - 1)], x_recv.at[7])
    dg_copy = pltpu.make_async_copy(dg_all, dg_out, out_sem.at[4])
    dg_copy.start()

    wait_bytes(qpart_in.at[pl.ds(0, PSG - 1)], recv_sem.at[4])
    qg_own[...] = jnp.sum(qpart_in[...].astype(F32), axis=0).astype(BF16)
    opposite = core * 4 + lax.rem(xpos + 2, 4)
    send(qg_own, qg_all.at[slot, me], side_send.at[0], side_recv.at[0], (me, pb_peers[4]))
    for to in far_first:
        send(qg_own, qg_all.at[slot, me], send_sem.at[5], recv_sem.at[7], (to, pb))
    qg_all[slot, me] = qg_own[...]
    wait_bytes(qg_own, side_recv.at[0])
    for to in far_first:
        send(qg_all.at[opposite, me], qg_all.at[opposite, me], send_sem.at[6], recv_sem.at[8], (to, pb))

    for k in (0, 4, 6, 5):
        wait_bytes(own, x_recv.at[k])
    o_copy = pltpu.make_async_copy(o_all, o_out, out_sem.at[5])
    o_copy.start()
    copies = []

    for i, count, ref in (
        (0, PSG - 1, partial), (1, PSG - 1, qa), (2, Y - 1, stats), (3, PSG - 1, g_all), (4, PSG - 1, qpart),
        (5, PSG - 1, qpart), (7, PSG - Y, stats),
    ):
        wait_bytes(ref.at[pl.ds(0, count)], send_sem.at[i])
    for k in range(7):
        wait_bytes(own, x_send.at[k])
    wait_bytes(dg_all.at[pl.ds(0, PB - 1)], x_send.at[7])
    wait_bytes(qg_own, side_send.at[0])
    for copy in (q_copy, probs_copy, g_copy, sgrad_copy, dg_copy, o_copy):
        copy.wait()

    def keep(at, first, count):
        part = pl.ds(first, count)
        copies.append(pltpu.make_async_copy(qg_all.at[at, part], qg_out.at[at, part], qg_sem.at[len(copies)]))
        copies[-1].start()

    def hand_over(at, first, count, k):
        part = qg_all.at[at, pl.ds(first, count)]
        send(part, part, core_send.at[k], core_recv.at[k], (me, partner))

    wait_bytes(qg_all.at[slot, pl.ds(0, PSG - 1)], recv_sem.at[7])
    for half in range(2):
        part = qg_all.at[slot, pl.ds(16 * half, 16)]
        for i, d in enumerate((2, 6)):
            send(part, part, side_send.at[1 + 2 * half + i], side_recv.at[1 + 2 * half + i], (me, pb_peers[d]))
    hand_over(slot, 0, PSG, 0)
    keep(slot, 0, PSG)
    wait_bytes(qg_all.at[slot, pl.ds(0, PSG - 1)], recv_sem.at[8])
    hand_over(opposite, 0, PSG, 1)
    keep(opposite, 0, PSG)
    sides = [core * 4 + lax.rem(xpos + d, 4) for d in (3, 1)]
    for half in range(2):
        for i in range(2):
            wait_bytes(qg_all.at[slot, pl.ds(0, 16)], side_recv.at[1 + 2 * half + i])
            hand_over(sides[i], 16 * half, 16, 2 + 2 * half + i)
    for i in range(2):
        keep(sides[i], 0, PSG)
    for k, d in enumerate((0, 2)):
        wait_bytes(qg_all.at[slot], core_recv.at[k])
        keep(lax.rem(slot + 4, PB) if d == 0 else lax.rem(opposite + 4, PB), 0, PSG)
    for half in range(2):
        for i in range(2):
            wait_bytes(qg_all.at[slot, pl.ds(0, 16)], core_recv.at[2 + 2 * half + i])
            keep(lax.rem(sides[i] + 4, PB), 16 * half, 16)

    wait_bytes(qpart.at[pl.ds(0, PSG - 1)], send_sem.at[6])
    for k in range(1, 5):
        wait_bytes(qg_all.at[slot, pl.ds(0, 16)], side_send.at[k])
    for k in range(6):
        wait_bytes(qg_all.at[slot, pl.ds(0, PSG if k < 2 else 16)], core_send.at[k])
    for copy in copies:
        copy.wait()


def grads_kernel(
    probs_hbm, sgrad_hbm, q_hbm, g_hbm, qg_hbm, o_hbm, dg_hbm, qw_hbm,
    hidden_hbm, kgrad_hbm, vgrad_hbm, qwg_hbm, owg_hbm,
    probs, sgrad, q, g_all, qg, o, dg, qw, hidden, kgrad, vgrad, qwg, owg, in_sem, out_sem,
):
    pb = lax.axis_index("pb")
    slot = (pb % 2) * 4 + pb // 2
    loads = {}

    def load(name, src, dst):
        loads[name] = pltpu.make_async_copy(src, dst, in_sem.at[len(loads)])
        loads[name].start()

    load("g", g_hbm, g_all)
    for g in range(0, GROUPS, 2):
        load(("p", g), probs_hbm.at[pl.ds(g, 2)], probs.at[pl.ds(g, 2)])
    load("q", q_hbm, q)
    for g in range(0, GROUPS, 2):
        load(("s", g), sgrad_hbm.at[pl.ds(g, 2)], sgrad.at[pl.ds(g, 2)])
    load("dg", dg_hbm, dg)
    load("o", o_hbm, o)
    load("qg", qg_hbm, qg)
    load("qw", qw_hbm, qw)

    stores = []

    def store(src, dst):
        stores.append(pltpu.make_async_copy(src, dst, out_sem.at[len(stores)]))
        stores[-1].start()

    def attention_grad(low, rows, out, out_hbm, key):
        for g in range(GROUPS):
            if g % 2 == 0:
                loads[key, g].wait()
            wide = pl.ds(g * 256, 256)
            out[:, wide] = dot(low[g], head_blocks(columns(rows[pl.ds(g * 4, 4)])), NN).astype(BF16)
            if g % 2 == 1:
                both = pl.ds((g - 1) * 256, 512)
                store(out.at[:, both], out_hbm.at[:, both])

    loads["g"].wait()
    attention_grad(probs, g_all, vgrad, vgrad_hbm, "p")
    loads["q"].wait()
    attention_grad(sgrad, q, kgrad, kgrad_hbm, "s")

    def all_questions(ref, g):
        return jnp.concatenate([columns(ref[s, pl.ds(g * 4, 4)]) for s in range(PB)], axis=0)

    loads["dg"].wait()
    loads["o"].wait()
    tokens = jnp.concatenate([dg[s, 1] for s in range(PB)], axis=0)
    for g in range(GROUPS):
        owg[g * 256 : (g + 1) * 256, :] = dot(all_questions(o, g), tokens, TN)
    store(owg, owg_hbm)
    loads["qg"].wait()
    tokens = jnp.concatenate([dg[s, 0] for s in range(PB)], axis=0)
    for g in range(GROUPS):
        qwg[:, g * 256 : (g + 1) * 256] = dot(tokens, all_questions(qg, g), TN)
    store(qwg, qwg_hbm)
    loads["qw"].wait()
    hidden[...] = sum(
        dot(columns(qg[slot, pl.ds(g * 4, 4)]), qw[:, g * 256 : (g + 1) * 256], NT) for g in range(GROUPS)
    ).astype(BF16)
    store(hidden, hidden_hbm)
    for copy in stores:
        copy.wait()


def local(
    dec_hidden, out_grad, query_weight, output_weight, queries, attn_out, row_max, row_sum, keys, values, lengths
):
    hbm = pl.BlockSpec(memory_space=pl.ANY)
    sds = jax.ShapeDtypeStruct
    pieces = (PSG, 16, 128)
    probs, sgrad, q_all, g_all, qg_all, o_all, dg_all = pl.pallas_call(
        comm_kernel,
        out_shape=[
            sds((GROUPS, 512, 128), BF16), sds((GROUPS, 512, 128), BF16), sds(pieces, BF16), sds(pieces, BF16),
            sds((PB,) + pieces, BF16), sds((PB,) + pieces, BF16), sds((PB, 2, 32, 128), BF16),
        ],
        in_specs=[hbm] * 10,
        out_specs=[hbm] * 7,
        scratch_shapes=[
            pltpu.VMEM((2048, 128), BF16),
            pltpu.VMEM((512, 2048), BF16),
            pltpu.VMEM((512, 2048), BF16),
            pltpu.VMEM((1, 2048), BF16),
            pltpu.VMEM((1, 2048), BF16),
            pltpu.VMEM((1, 32), F32),
            pltpu.VMEM((1, 32), F32),
            pltpu.SMEM((1, 2), jnp.int32),
            pltpu.VMEM((32, 128), F32),
            pltpu.VMEM((PSG, 32, 128), BF16),
            pltpu.VMEM((PSG, 32, 128), F32),
            pltpu.VMEM((1, 128), F32),
            pltpu.VMEM((PSG, 1, 128), F32),
            pltpu.VMEM(pieces, BF16),
            pltpu.VMEM(pieces, BF16),
            pltpu.VMEM((16, 128), BF16),
            pltpu.VMEM(pieces, BF16),
            pltpu.VMEM(pieces, BF16),
            pltpu.VMEM((GROUPS, 512, 128), F32),
            pltpu.VMEM((GROUPS, 512, 128), BF16),
            pltpu.VMEM((GROUPS, 512, 128), BF16),
            pltpu.VMEM(pieces, BF16),
            pltpu.VMEM(pieces, BF16),
            pltpu.VMEM((16, 128), BF16),
            pltpu.VMEM((PB,) + pieces, BF16),
            pltpu.VMEM((PB,) + pieces, BF16),
            pltpu.VMEM((2, 32, 128), BF16),
            pltpu.VMEM((PB, 2, 32, 128), BF16),
            pltpu.SemaphoreType.DMA((10,)),
            pltpu.SemaphoreType.DMA((9,)),
            pltpu.SemaphoreType.DMA((9,)),
            pltpu.SemaphoreType.DMA((8,)),
            pltpu.SemaphoreType.DMA((8,)),
            pltpu.SemaphoreType.DMA((5,)),
            pltpu.SemaphoreType.DMA((5,)),
            pltpu.SemaphoreType.DMA((6,)),
            pltpu.SemaphoreType.DMA((6,)),
            pltpu.SemaphoreType.DMA((6,)),
            pltpu.SemaphoreType.DMA((10,)),
        ],
        compiler_params=pltpu.CompilerParams(collective_id=1, has_side_effects=True, vmem_limit_bytes=62 * 2**20),
        cost_estimate=pl.CostEstimate(flops=10**9, bytes_accessed=10**7, transcendentals=512 * 1024),
        name="comm",
    )(
        dec_hidden.reshape(32, 128), out_grad.reshape(32, 128), output_weight,
        queries.reshape(1, 2048), attn_out.reshape(1, 2048), row_max.reshape(1, 32), row_sum.reshape(1, 32),
        keys.reshape(512, 2048), values.reshape(512, 2048), lengths,
    )

    hidden, kgrad, vgrad, qwg, owg = pl.pallas_call(
        grads_kernel,
        out_shape=[
            sds((32, 128), BF16), sds((512, 2048), BF16), sds((512, 2048), BF16),
            sds((128, 2048), F32), sds((2048, 128), F32),
        ],
        in_specs=[hbm] * 8,
        out_specs=[hbm] * 5,
        scratch_shapes=[
            pltpu.VMEM((GROUPS, 512, 128), BF16),
            pltpu.VMEM((GROUPS, 512, 128), BF16),
            pltpu.VMEM(pieces, BF16),
            pltpu.VMEM(pieces, BF16),
            pltpu.VMEM((PB,) + pieces, BF16),
            pltpu.VMEM((PB,) + pieces, BF16),
            pltpu.VMEM((PB, 2, 32, 128), BF16),
            pltpu.VMEM((128, 2048), BF16),
            pltpu.VMEM((32, 128), BF16),
            pltpu.VMEM((512, 2048), BF16),
            pltpu.VMEM((512, 2048), BF16),
            pltpu.VMEM((128, 2048), F32),
            pltpu.VMEM((2048, 128), F32),
            pltpu.SemaphoreType.DMA((14,)),
            pltpu.SemaphoreType.DMA((11,)),
        ],
        compiler_params=pltpu.CompilerParams(vmem_limit_bytes=62 * 2**20),
        cost_estimate=pl.CostEstimate(flops=10**9, bytes_accessed=10**7, transcendentals=0),
        name="grads",
    )(probs, sgrad, q_all, g_all, qg_all, o_all, dg_all, query_weight)
    return (
        hidden.reshape(dec_hidden.shape), kgrad.reshape(keys.shape), vgrad.reshape(values.shape), qwg, owg
    )


def solution(mesh):
    in_specs = (
        P("pb", None, "psg"),
        P("pb", None, "psg"),
        P("psg", None),
        P(None, "psg"),
        P("pb", "psg", None),
        P("pb", "psg", None),
        P("pb", "psg", None),
        P("pb", "psg", None),
        P("pb", "psg", None, None),
        P("pb", "psg", None, None),
        P("pb", "psg"),
    )
    out_specs = (
        P("pb", None, "psg"),
        P("pb", "psg", None, None),
        P("pb", "psg", None, None),
        P("psg", None),
        P(None, "psg"),
    )
    return jax.shard_map(local, mesh=mesh, in_specs=in_specs, out_specs=out_specs, check_vma=False)
```

```python
import jax
import jax.numpy as jnp
from jax import lax
from jax.experimental import pallas as pl
from jax.experimental.pallas import tpu as pltpu
from jax.sharding import PartitionSpec as P

MESH = pl.DeviceIdType.MESH
F32 = jnp.float32
BF16 = jnp.bfloat16

NT = (((1,), (1,)), ((), ()))
TN = (((0,), (0,)), ((), ()))
NN = (((1,), (0,)), ((), ()))

Z, Y, PSG, PB = 8, 4, 32, 8
GROUPS = 8
NEAR = (0, 1, 7, 2, 6, 3, 5, 4)


def dot(a, b, dims):
    return lax.dot_general(a, b, dims, preferred_element_type=F32)


def columns(pieces):
    left = jnp.concatenate([pieces[0], pieces[1]], axis=0)
    right = jnp.concatenate([pieces[2], pieces[3]], axis=0)
    return jnp.concatenate([left, right], axis=1)


def head_blocks(rows):
    tiled = jnp.concatenate([rows] * 4, axis=0)
    row = lax.broadcasted_iota(jnp.int32, tiled.shape, 0) // 32
    col = lax.broadcasted_iota(jnp.int32, tiled.shape, 1) // 64
    return jnp.where(row == col, tiled, jnp.zeros_like(tiled))


def split_bf16(x, terms):
    out = []
    for _ in range(terms):
        part = x.astype(BF16)
        out.append(part)
        x = x - part.astype(F32)
    return out


def comm_kernel(
    dec_hbm, grad_hbm, weight_hbm, query_hbm, attn_hbm, max_hbm, sum_hbm, keys_hbm, values_hbm, len_hbm,
    kgrad_out, vgrad_out, owg_out, qg_out, dg_out, q_out,
    weight, keys, values, query_ref, attn_ref, max_ref, sum_ref, len_ref, bundle, qa, qa32, stat_src, stats,
    partial, part_in, g_own, g_all, q_all, probs, probs_low, sgrad, vgrad, owg, qpart, qpart_in, qg_own, qg_all,
    o_all, dg_src, dg_all,
    local_sem, send_sem, recv_sem, x_send, x_recv, side_send, side_recv, core_send,
    core_recv, out_sem,
):
    me, pb = lax.axis_index("psg"), lax.axis_index("pb")
    z, y = lax.div(me, Y), lax.rem(me, Y)
    half_of = lax.div(z, 4)
    core, xpos = lax.rem(pb, 2), lax.div(pb, 2)
    slot = core * 4 + xpos
    partner = pb + 1 - 2 * core
    zs = [lax.rem(z + d, Z) for d in range(Z)]
    ys = [lax.rem(y + d, Y) for d in range(Y)]
    peers = {(dz, dy): zs[dz] * Y + ys[dy] for dz in range(Z) for dy in range(Y) if dz or dy}
    far_first = [peers[dz, dy] for dz in reversed(NEAR) for dy in (2, 1, 3, 0) if dz or dy]
    pb_peers = [lax.rem(pb + d, PB) for d in range(PB)]

    barrier = pltpu.get_barrier_semaphore()
    for to in far_first:
        pl.semaphore_signal(barrier, inc=1, device_id=(to, pb), device_id_type=MESH)
    for d in range(1, PB):
        pl.semaphore_signal(barrier, inc=1, device_id=(me, pb_peers[d]), device_id_type=MESH)

    loads = [
        pltpu.make_async_copy(src, dst, local_sem.at[i])
        for i, (src, dst) in enumerate((
            (query_hbm, query_ref), (attn_hbm, attn_ref), (max_hbm, max_ref), (sum_hbm, sum_ref),
            (dec_hbm, dg_src.at[0]), (grad_hbm, dg_src.at[1]), (weight_hbm, weight), (len_hbm, len_ref),
            (keys_hbm, keys), (values_hbm, values),
        ))
    ]
    for load in loads:
        load.start()
    keys_copy, values_copy = loads[8:]
    for load in loads[:6]:
        load.wait()

    for k in range(16):
        bundle[k : k + 1, :] = query_ref[:, k * 128 : (k + 1) * 128].astype(F32)
        bundle[16 + k : 17 + k, :] = attn_ref[:, k * 128 : (k + 1) * 128].astype(F32)
    qa[me] = bundle[...].astype(BF16)
    stat_src[...] = jnp.zeros_like(stat_src)
    stat_src[0:1, 0:32] = max_ref[...] + jnp.log(sum_ref[...])
    stats[me] = stat_src[...]
    dg_all[slot] = dg_src[...]

    loads[6].wait()
    loads[7].wait()
    grad = dg_src[1]
    for k in range(16):
        block = dot(grad, weight[k * 128 : (k + 1) * 128, :], NT).astype(BF16)
        partial[2 * k] = block[0:16]
        partial[2 * k + 1] = block[16:32]

    pl.semaphore_wait(barrier, PSG - 1 + PB - 1)

    def send(src, dst, send_at, recv_at, to):
        pltpu.make_async_remote_copy(
            src_ref=src, dst_ref=dst, send_sem=send_at, recv_sem=recv_at, device_id=to, device_id_type=MESH
        ).start()

    def wait_bytes(ref, sem):
        pltpu.make_async_copy(ref, ref, sem).wait()

    for to in far_first:
        send(partial.at[to], part_in.at[me], send_sem.at[0], recv_sem.at[0], (to, pb))
    part_in[me] = partial[me]
    for dy in (2, 1, 3):
        send(stats.at[me], stats.at[me], send_sem.at[2], recv_sem.at[2], (peers[0, dy], pb))
    for to in far_first:
        send(qa.at[me], qa.at[me], send_sem.at[1], recv_sem.at[1], (to, pb))
    row_of_four = pl.ds(z * Y, Y)
    wait_bytes(stats.at[pl.ds(0, Y - 1)], recv_sem.at[2])
    for dz in (4, 5, 3, 6, 2, 7, 1):
        send(stats.at[row_of_four], stats.at[row_of_four], send_sem.at[7], recv_sem.at[5], (peers[dz, 0], pb))

    wait_bytes(part_in.at[pl.ds(0, PSG - 1)], recv_sem.at[0])
    g_own[...] = jnp.sum(part_in[...].astype(F32), axis=0).astype(BF16)
    for to in far_first:
        send(g_own, g_all.at[me], send_sem.at[3], recv_sem.at[3], (to, pb))
    g_all[me] = g_own[...]
    for d in range(1, PB):
        send(dg_src, dg_all.at[slot], x_send.at[1], x_recv.at[4], (me, pb_peers[d]))

    wait_bytes(qa.at[pl.ds(0, PSG - 1)], recv_sem.at[1])
    qa32[...] = qa[...].astype(F32)
    for k in range(16):
        block = qa32[:, k, :].astype(BF16)
        q_all[2 * k] = block[0:16]
        q_all[2 * k + 1] = block[16:32]
        block = qa32[:, 16 + k, :].astype(BF16)
        o_all[slot, 2 * k] = block[0:16]
        o_all[slot, 2 * k + 1] = block[16:32]
    own = o_all.at[slot]
    for d in range(1, 4):
        send(own, own, x_send.at[0], x_recv.at[d], (me, pb_peers[2 * d]))
    send(own, own, x_send.at[0], x_recv.at[0], (me, partner))

    wait_bytes(stats.at[pl.ds(0, PSG - Y)], recv_sem.at[5])
    stat_rows = jnp.concatenate([stats[t] for t in range(PSG)], axis=0)
    head = lax.broadcasted_iota(jnp.int32, (128, 1024), 0)
    lane = lax.broadcasted_iota(jnp.int32, (128, 1024), 1)
    pick = jnp.where(head == lane // 32, 1.0, 0.0).astype(BF16)
    spread = sum(dot(part, pick, NN) for part in split_bf16(stat_rows, 3))
    token = lax.broadcasted_iota(jnp.int32, (32, 1024), 0)
    lane = lax.broadcasted_iota(jnp.int32, (32, 1024), 1)
    stat_lanes = jnp.sum(jnp.where(token == lane % 32, spread, 0.0), axis=0, keepdims=True)

    keys_copy.wait()
    position = lax.broadcasted_iota(jnp.int32, (256, 128), 0)
    for g in range(GROUPS):
        blocks = head_blocks(columns(q_all[pl.ds(g * 4, 4)]))
        scores = dot(keys[:, g * 256 : (g + 1) * 256], blocks, NT) - stat_lanes[:, g * 128 : (g + 1) * 128]
        for p in range(2):
            rows = pl.ds(p * 256, 256)
            value = jnp.where(position < len_ref[0, p], jnp.exp(scores[p * 256 : (p + 1) * 256]), 0.0)
            probs[g, rows] = value
            probs_low[g, rows] = value.astype(BF16)
    values_copy.wait()

    wait_bytes(g_all.at[pl.ds(0, PSG - 1)], recv_sem.at[3])
    ones = jnp.ones((8, 256), BF16)
    for g in range(GROUPS):
        four = pl.ds(g * 4, 4)
        blocks = head_blocks(columns(g_all[four]))
        out_rows = columns(o_all[slot, four]).astype(F32)
        product = blocks.astype(F32) * jnp.concatenate([out_rows] * 4, axis=0)
        delta = sum(dot(ones, part, NT) for part in split_bf16(product, 2))[0:1]
        prob_grad = dot(values[:, g * 256 : (g + 1) * 256], blocks, NT)
        sgrad[g] = (probs[g] * (prob_grad - delta)).astype(BF16)
    row = lax.broadcasted_iota(jnp.int32, (128, 256), 0) // 32
    col = lax.broadcasted_iota(jnp.int32, (128, 256), 1) // 64
    for g in range(GROUPS):
        part = jnp.where(row == col, dot(sgrad[g], keys[:, g * 256 : (g + 1) * 256], TN), 0.0)
        part = (part[0:32] + part[32:64] + part[64:96] + part[96:128]).astype(BF16)
        qpart[g * 4] = part[0:16, 0:128]
        qpart[g * 4 + 1] = part[16:32, 0:128]
        qpart[g * 4 + 2] = part[0:16, 128:256]
        qpart[g * 4 + 3] = part[16:32, 128:256]
    for to in far_first:
        send(qpart.at[to], qpart_in.at[me], send_sem.at[4], recv_sem.at[4], (to, pb))
    qpart_in[me] = qpart[me]

    for g in range(GROUPS):
        wide, four = pl.ds(g * 256, 256), pl.ds(g * 4, 4)
        vgrad[:, wide] = dot(probs_low[g], head_blocks(columns(g_all[four])), NN).astype(BF16)
    vgrad_copy = pltpu.make_async_copy(vgrad, vgrad_out, out_sem.at[0])
    vgrad_copy.start()
    kgrad_copy = pltpu.make_async_copy(sgrad, kgrad_out, out_sem.at[1])
    kgrad_copy.start()
    q_copy = pltpu.make_async_copy(q_all, q_out, out_sem.at[5])
    q_copy.start()

    for d in (1, 3, 2):
        wait_bytes(own, x_recv.at[d])
        got = o_all.at[core * 4 + lax.rem(xpos + 4 - d, 4)]
        send(got, got, x_send.at[0], x_recv.at[0], (me, partner))
    wait_bytes(dg_all.at[pl.ds(0, PB - 1)], x_recv.at[4])
    dg_copy = pltpu.make_async_copy(dg_all, dg_out, out_sem.at[2])
    dg_copy.start()

    wait_bytes(qpart_in.at[pl.ds(0, PSG - 1)], recv_sem.at[4])
    qg_own[...] = jnp.sum(qpart_in[...].astype(F32), axis=0).astype(BF16)
    opposite = core * 4 + lax.rem(xpos + 2, 4)
    send(qg_own, qg_all.at[slot, me], side_send.at[0], side_recv.at[0], (me, pb_peers[4]))
    for to in far_first:
        send(qg_own, qg_all.at[slot, me], send_sem.at[5], recv_sem.at[6 + half_of], (to, pb))
    qg_all[slot, me] = qg_own[...]
    wait_bytes(qg_own, side_recv.at[0])
    for to in far_first:
        send(qg_all.at[opposite, me], qg_all.at[opposite, me], send_sem.at[6], recv_sem.at[8], (to, pb))

    wait_bytes(o_all.at[pl.ds(0, 4)], x_recv.at[0])
    tokens = jnp.concatenate([dg_all[s, 1] for s in range(PB)], axis=0)
    for g in range(GROUPS):
        rows = jnp.concatenate([columns(o_all[s, pl.ds(g * 4, 4)]) for s in range(PB)], axis=0)
        owg[g * 256 : (g + 1) * 256, :] = dot(rows, tokens, TN)
    owg_copy = pltpu.make_async_copy(owg, owg_out, out_sem.at[3])
    owg_copy.start()
    for i, count, ref in (
        (0, PSG - 1, partial), (1, PSG - 1, qa), (2, Y - 1, stats), (3, PSG - 1, g_all), (4, PSG - 1, qpart),
        (5, PSG - 1, qpart), (7, PSG - Y, stats),
    ):
        wait_bytes(ref.at[pl.ds(0, count)], send_sem.at[i])
    wait_bytes(o_all.at[pl.ds(0, 7)], x_send.at[0])
    wait_bytes(dg_all.at[pl.ds(0, PB - 1)], x_send.at[1])
    wait_bytes(qg_own, side_send.at[0])
    for copy in (vgrad_copy, kgrad_copy, dg_copy, owg_copy, q_copy):
        copy.wait()

    def keep(at):
        pltpu.make_async_copy(qg_all.at[at], qg_out.at[at], out_sem.at[5]).start()

    def hand_over(at, first, count):
        part = pl.ds(first, count)
        send(qg_all.at[at, part], qg_out.at[at, part], core_send.at[0], core_recv.at[0], (me, partner))

    firsts = (16 * half_of, 16 - 16 * half_of)
    for half, first in enumerate(firsts):
        wait_bytes(qg_all.at[slot, pl.ds(0, 15 + half)], recv_sem.at[6 + half_of if half == 0 else 7 - half_of])
        part = qg_all.at[slot, pl.ds(first, 16)]
        for d in (2, 6):
            send(part, part, side_send.at[1], side_recv.at[1 + half], (me, pb_peers[d]))
    hand_over(slot, 0, PSG)
    keep(slot)
    wait_bytes(qg_all.at[slot, pl.ds(0, PSG - 1)], recv_sem.at[8])
    hand_over(opposite, 0, PSG)
    keep(opposite)
    sides = [core * 4 + lax.rem(xpos + d, 4) for d in (3, 1)]
    for half in range(2):
        wait_bytes(qg_all.at[slot], side_recv.at[1 + half])
        for at in sides:
            hand_over(at, firsts[half], 16)
    for at in sides:
        keep(at)
    wait_bytes(qpart.at[pl.ds(0, PSG - 1)], send_sem.at[6])
    wait_bytes(qg_all.at[pl.ds(0, 2)], side_send.at[1])
    wait_bytes(qg_all.at[pl.ds(0, 4)], core_send.at[0])
    wait_bytes(qg_all.at[pl.ds(0, 4)], out_sem.at[5])
    wait_bytes(qg_all.at[pl.ds(0, 4)], core_recv.at[0])


def grads_kernel(
    kgrad_in, vgrad_in, owg_in, qg_hbm, dg_hbm, qw_hbm, q_hbm, hidden_hbm, kgrad_out, vgrad_out, qwg_hbm, owg_out,
    sgrad, kgrad, vgrad, owg, qg, dg, qw, q_all, hidden, qwg, in_sem, out_sem,
):
    pb = lax.axis_index("pb")
    slot = (pb % 2) * 4 + pb // 2
    loads = []

    def load(src, dst):
        loads.append(pltpu.make_async_copy(src, dst, in_sem.at[len(loads)]))
        loads[-1].start()
        return loads[-1]

    def store(i, src, dst):
        pltpu.make_async_copy(src, dst, out_sem.at[i]).start()

    q_load = load(q_hbm, q_all)
    k_loads = [load(kgrad_in.at[pl.ds(g, 2)], sgrad.at[pl.ds(g, 2)]) for g in range(0, GROUPS, 2)]
    v_loads = [load(vgrad_in.at[pl.ds(i * 256, 256)], vgrad.at[pl.ds(i * 256, 256)]) for i in range(2)]
    dg_load = load(dg_hbm, dg)
    qg_load = load(qg_hbm, qg)
    qw_load = load(qw_hbm, qw)
    owg_load = load(owg_in, owg)

    q_load.wait()
    for g in range(GROUPS):
        if g % 2 == 0:
            k_loads[g // 2].wait()
        wide, four = pl.ds(g * 256, 256), pl.ds(g * 4, 4)
        kgrad[:, wide] = dot(sgrad[g], head_blocks(columns(q_all[four])), NN).astype(BF16)
        if g % 2 == 1:
            both = pl.ds((g - 1) * 256, 512)
            store(1, kgrad.at[:, both], kgrad_out.at[:, both])
    for i in range(2):
        rows = pl.ds(i * 256, 256)
        v_loads[i].wait()
        store(0, vgrad.at[rows], vgrad_out.at[rows])
    dg_load.wait()
    qg_load.wait()
    tokens = jnp.concatenate([dg[s, 0] for s in range(PB)], axis=0)
    for g in range(GROUPS):
        wide, four = pl.ds(g * 256, 256), pl.ds(g * 4, 4)
        qwg[:, wide] = dot(tokens, jnp.concatenate([columns(qg[s, four]) for s in range(PB)], axis=0), TN)
        if g % 4 == 3:
            half = pl.ds((g - 3) * 256, 1024)
            store(2, qwg.at[:, half], qwg_hbm.at[:, half])
    owg_load.wait()
    store(3, owg, owg_out)
    qw_load.wait()
    hidden[...] = sum(
        dot(columns(qg[slot, pl.ds(g * 4, 4)]), qw[:, g * 256 : (g + 1) * 256], NT) for g in range(GROUPS)
    ).astype(BF16)
    store(4, hidden, hidden_hbm)
    for i, ref in enumerate((vgrad, kgrad, qwg, owg, hidden)):
        pltpu.make_async_copy(ref, ref, out_sem.at[i]).wait()


def local(
    dec_hidden, out_grad, query_weight, output_weight, queries, attn_out, row_max, row_sum, keys, values, lengths
):
    hbm = pl.BlockSpec(memory_space=pl.ANY)
    sds = jax.ShapeDtypeStruct
    pieces = (PSG, 16, 128)
    kgrad, vgrad, owg, qg_all, dg_all, q_all = pl.pallas_call(
        comm_kernel,
        out_shape=[
            sds((GROUPS, 512, 128), BF16), sds((512, 2048), BF16), sds((2048, 128), F32),
            sds((PB,) + pieces, BF16), sds((PB, 2, 32, 128), BF16), sds(pieces, BF16),
        ],
        in_specs=[hbm] * 10,
        out_specs=[hbm] * 6,
        scratch_shapes=[
            pltpu.VMEM((2048, 128), BF16),
            pltpu.VMEM((512, 2048), BF16),
            pltpu.VMEM((512, 2048), BF16),
            pltpu.VMEM((1, 2048), BF16),
            pltpu.VMEM((1, 2048), BF16),
            pltpu.VMEM((1, 32), F32),
            pltpu.VMEM((1, 32), F32),
            pltpu.SMEM((1, 2), jnp.int32),
            pltpu.VMEM((32, 128), F32),
            pltpu.VMEM((PSG, 32, 128), BF16),
            pltpu.VMEM((PSG, 32, 128), F32),
            pltpu.VMEM((1, 128), F32),
            pltpu.VMEM((PSG, 1, 128), F32),
            pltpu.VMEM(pieces, BF16),
            pltpu.VMEM(pieces, BF16),
            pltpu.VMEM((16, 128), BF16),
            pltpu.VMEM(pieces, BF16),
            pltpu.VMEM(pieces, BF16),
            pltpu.VMEM((GROUPS, 512, 128), F32),
            pltpu.VMEM((GROUPS, 512, 128), BF16),
            pltpu.VMEM((GROUPS, 512, 128), BF16),
            pltpu.VMEM((512, 2048), BF16),
            pltpu.VMEM((2048, 128), F32),
            pltpu.VMEM(pieces, BF16),
            pltpu.VMEM(pieces, BF16),
            pltpu.VMEM((16, 128), BF16),
            pltpu.VMEM((PB,) + pieces, BF16),
            pltpu.VMEM((PB,) + pieces, BF16),
            pltpu.VMEM((2, 32, 128), BF16),
            pltpu.VMEM((PB, 2, 32, 128), BF16),
            pltpu.SemaphoreType.DMA((10,)),
            pltpu.SemaphoreType.DMA((8,)),
            pltpu.SemaphoreType.DMA((9,)),
            pltpu.SemaphoreType.DMA((2,)),
            pltpu.SemaphoreType.DMA((5,)),
            pltpu.SemaphoreType.DMA((2,)),
            pltpu.SemaphoreType.DMA((3,)),
            pltpu.SemaphoreType.DMA((1,)),
            pltpu.SemaphoreType.DMA((1,)),
            pltpu.SemaphoreType.DMA((6,)),
        ],
        compiler_params=pltpu.CompilerParams(collective_id=1, has_side_effects=True, vmem_limit_bytes=62 * 2**20),
        cost_estimate=pl.CostEstimate(flops=10**9, bytes_accessed=10**7, transcendentals=512 * 1024),
        name="comm",
    )(
        dec_hidden.reshape(32, 128), out_grad.reshape(32, 128), output_weight,
        queries.reshape(1, 2048), attn_out.reshape(1, 2048), row_max.reshape(1, 32), row_sum.reshape(1, 32),
        keys.reshape(512, 2048), values.reshape(512, 2048), lengths,
    )

    hidden, kgrad, vgrad, qwg, owg = pl.pallas_call(
        grads_kernel,
        out_shape=[
            sds((32, 128), BF16), sds((512, 2048), BF16), sds((512, 2048), BF16),
            sds((128, 2048), F32), sds((2048, 128), F32),
        ],
        in_specs=[hbm] * 7,
        out_specs=[hbm] * 5,
        scratch_shapes=[
            pltpu.VMEM((GROUPS, 512, 128), BF16),
            pltpu.VMEM((512, 2048), BF16),
            pltpu.VMEM((512, 2048), BF16),
            pltpu.VMEM((2048, 128), F32),
            pltpu.VMEM((PB,) + pieces, BF16),
            pltpu.VMEM((PB, 2, 32, 128), BF16),
            pltpu.VMEM((128, 2048), BF16),
            pltpu.VMEM(pieces, BF16),
            pltpu.VMEM((32, 128), BF16),
            pltpu.VMEM((128, 2048), F32),
            pltpu.SemaphoreType.DMA((14,)),
            pltpu.SemaphoreType.DMA((5,)),
        ],
        compiler_params=pltpu.CompilerParams(vmem_limit_bytes=62 * 2**20),
        cost_estimate=pl.CostEstimate(flops=10**9, bytes_accessed=10**7, transcendentals=0),
        name="grads",
    )(kgrad, vgrad, owg, qg_all, dg_all, query_weight, q_all)
    return (
        hidden.reshape(dec_hidden.shape), kgrad.reshape(keys.shape), vgrad.reshape(values.shape), qwg, owg
    )


def solution(mesh):
    in_specs = (
        P("pb", None, "psg"),
        P("pb", None, "psg"),
        P("psg", None),
        P(None, "psg"),
        P("pb", "psg", None),
        P("pb", "psg", None),
        P("pb", "psg", None),
        P("pb", "psg", None),
        P("pb", "psg", None, None),
        P("pb", "psg", None, None),
        P("pb", "psg"),
    )
    out_specs = (
        P("pb", None, "psg"),
        P("pb", "psg", None, None),
        P("pb", "psg", None, None),
        P("psg", None),
        P(None, "psg"),
    )
    return jax.shard_map(local, mesh=mesh, in_specs=in_specs, out_specs=out_specs, check_vma=False)
```

```python
import jax
import jax.numpy as jnp
from jax import lax
from jax.experimental import pallas as pl
from jax.experimental.pallas import tpu as pltpu
from jax.sharding import PartitionSpec as P

MESH = pl.DeviceIdType.MESH
F32 = jnp.float32
BF16 = jnp.bfloat16

NT = (((1,), (1,)), ((), ()))
TN = (((0,), (0,)), ((), ()))
NN = (((1,), (0,)), ((), ()))

Z, Y, PSG, PB = 8, 4, 32, 8
GROUPS = 8
NEAR = (0, 1, 7, 2, 6, 3, 5, 4)


def dot(a, b, dims):
    return lax.dot_general(a, b, dims, preferred_element_type=F32)


def columns(pieces):
    left = jnp.concatenate([pieces[0], pieces[1]], axis=0)
    right = jnp.concatenate([pieces[2], pieces[3]], axis=0)
    return jnp.concatenate([left, right], axis=1)


def head_blocks(rows):
    tiled = jnp.concatenate([rows] * 4, axis=0)
    row = lax.broadcasted_iota(jnp.int32, tiled.shape, 0) // 32
    col = lax.broadcasted_iota(jnp.int32, tiled.shape, 1) // 64
    return jnp.where(row == col, tiled, jnp.zeros_like(tiled))


def split_bf16(x, terms):
    out = []
    for _ in range(terms):
        part = x.astype(BF16)
        out.append(part)
        x = x - part.astype(F32)
    return out


def comm_kernel(
    dec_hbm, grad_hbm, weight_hbm, query_hbm, attn_hbm, max_hbm, sum_hbm, keys_hbm, values_hbm, len_hbm,
    kgrad_out, vgrad_out, owg_out, qg_out, dg_out, q_out,
    weight, keys, values, query_ref, attn_ref, max_ref, sum_ref, len_ref, bundle, qa, qa32, stat_src, stats,
    partial, part_in, g_own, g_all, q_all, probs, probs_low, sgrad, vgrad, owg, qpart, qpart_in, qg_own, qg_all,
    o_all, dg_src, dg_all,
    local_sem, send_sem, recv_sem, x_send, x_recv, side_send, side_recv, core_send,
    core_recv, out_sem,
):
    me, pb = lax.axis_index("psg"), lax.axis_index("pb")
    z, y = lax.div(me, Y), lax.rem(me, Y)
    half_of = lax.div(z, 4)
    core, xpos = lax.rem(pb, 2), lax.div(pb, 2)
    slot = core * 4 + xpos
    partner = pb + 1 - 2 * core
    zs = [lax.rem(z + d, Z) for d in range(Z)]
    ys = [lax.rem(y + d, Y) for d in range(Y)]
    peers = {(dz, dy): zs[dz] * Y + ys[dy] for dz in range(Z) for dy in range(Y) if dz or dy}
    far_first = [peers[dz, dy] for dz in reversed(NEAR) for dy in (2, 1, 3, 0) if dz or dy]
    pb_peers = [lax.rem(pb + d, PB) for d in range(PB)]

    barrier = pltpu.get_barrier_semaphore()
    for to in far_first:
        pl.semaphore_signal(barrier, inc=1, device_id=(to, pb), device_id_type=MESH)
    for d in range(1, PB):
        pl.semaphore_signal(barrier, inc=1, device_id=(me, pb_peers[d]), device_id_type=MESH)

    loads = [
        pltpu.make_async_copy(src, dst, local_sem.at[i])
        for i, (src, dst) in enumerate((
            (query_hbm, query_ref), (attn_hbm, attn_ref), (max_hbm, max_ref), (sum_hbm, sum_ref),
            (dec_hbm, dg_src.at[0]), (grad_hbm, dg_src.at[1]), (weight_hbm, weight), (len_hbm, len_ref),
            (keys_hbm, keys), (values_hbm, values),
        ))
    ]
    for load in loads:
        load.start()
    keys_copy, values_copy = loads[8:]
    for load in loads[:6]:
        load.wait()

    for k in range(16):
        bundle[k : k + 1, :] = query_ref[:, k * 128 : (k + 1) * 128].astype(F32)
        bundle[16 + k : 17 + k, :] = attn_ref[:, k * 128 : (k + 1) * 128].astype(F32)
    qa[0, me] = bundle[0:16].astype(BF16)
    qa[1, me] = bundle[16:32].astype(BF16)
    stat_src[...] = jnp.zeros_like(stat_src)
    stat_src[0:1, 0:32] = max_ref[...] + jnp.log(sum_ref[...])
    stats[me] = stat_src[...]
    dg_all[slot] = dg_src[...]

    loads[6].wait()
    loads[7].wait()
    grad = dg_src[1]
    for k in range(16):
        block = dot(grad, weight[k * 128 : (k + 1) * 128, :], NT).astype(BF16)
        partial[2 * k] = block[0:16]
        partial[2 * k + 1] = block[16:32]

    pl.semaphore_wait(barrier, PSG - 1 + PB - 1)

    def send(src, dst, send_at, recv_at, to):
        pltpu.make_async_remote_copy(
            src_ref=src, dst_ref=dst, send_sem=send_at, recv_sem=recv_at, device_id=to, device_id_type=MESH
        ).start()

    def wait_bytes(ref, sem):
        pltpu.make_async_copy(ref, ref, sem).wait()

    for to in far_first:
        send(partial.at[to], part_in.at[me], send_sem.at[0], recv_sem.at[0], (to, pb))
    part_in[me] = partial[me]
    for dy in (2, 1, 3):
        send(qa.at[1, me], qa.at[1, me], send_sem.at[8], recv_sem.at[9], (peers[0, dy], pb))
        send(stats.at[me], stats.at[me], send_sem.at[2], recv_sem.at[2], (peers[0, dy], pb))
    for to in far_first:
        send(qa.at[0, me], qa.at[0, me], send_sem.at[1], recv_sem.at[1], (to, pb))
    row_of_four = pl.ds(z * Y, Y)
    wait_bytes(stats.at[pl.ds(0, Y - 1)], recv_sem.at[2])
    for dz in (4, 5, 3, 6, 2, 7, 1):
        send(stats.at[row_of_four], stats.at[row_of_four], send_sem.at[7], recv_sem.at[5], (peers[dz, 0], pb))

    wait_bytes(part_in.at[pl.ds(0, PSG - 1)], recv_sem.at[0])
    g_own[...] = jnp.sum(part_in[...].astype(F32), axis=0).astype(BF16)
    for to in far_first:
        send(g_own, g_all.at[me], send_sem.at[3], recv_sem.at[3], (to, pb))
    g_all[me] = g_own[...]
    wait_bytes(qa.at[1, pl.ds(0, Y - 1)], recv_sem.at[9])
    for dz in (4, 5, 3, 6, 2, 7, 1):
        rows = qa.at[1, row_of_four]
        send(rows, rows, send_sem.at[9], recv_sem.at[10], (peers[dz, 0], pb))
    for d in range(1, PB):
        send(dg_src, dg_all.at[slot], x_send.at[1], x_recv.at[4], (me, pb_peers[d]))

    wait_bytes(qa.at[0, pl.ds(0, PSG - 1)], recv_sem.at[1])
    qa32[...] = qa[0].astype(F32)
    for k in range(16):
        block = qa32[:, k, :].astype(BF16)
        q_all[2 * k] = block[0:16]
        q_all[2 * k + 1] = block[16:32]

    wait_bytes(stats.at[pl.ds(0, PSG - Y)], recv_sem.at[5])
    stat_rows = jnp.concatenate([stats[t] for t in range(PSG)], axis=0)
    head = lax.broadcasted_iota(jnp.int32, (128, 1024), 0)
    lane = lax.broadcasted_iota(jnp.int32, (128, 1024), 1)
    pick = jnp.where(head == lane // 32, 1.0, 0.0).astype(BF16)
    spread = sum(dot(part, pick, NN) for part in split_bf16(stat_rows, 3))
    token = lax.broadcasted_iota(jnp.int32, (32, 1024), 0)
    lane = lax.broadcasted_iota(jnp.int32, (32, 1024), 1)
    stat_lanes = jnp.sum(jnp.where(token == lane % 32, spread, 0.0), axis=0, keepdims=True)

    keys_copy.wait()
    position = lax.broadcasted_iota(jnp.int32, (256, 128), 0)
    for g in range(GROUPS):
        blocks = head_blocks(columns(q_all[pl.ds(g * 4, 4)]))
        scores = dot(keys[:, g * 256 : (g + 1) * 256], blocks, NT) - stat_lanes[:, g * 128 : (g + 1) * 128]
        for p in range(2):
            rows = pl.ds(p * 256, 256)
            value = jnp.where(position < len_ref[0, p], jnp.exp(scores[p * 256 : (p + 1) * 256]), 0.0)
            probs[g, rows] = value
            probs_low[g, rows] = value.astype(BF16)
    wait_bytes(qa.at[1, pl.ds(0, PSG - Y)], recv_sem.at[10])
    qa32[...] = qa[1].astype(F32)
    for k in range(16):
        block = qa32[:, k, :].astype(BF16)
        o_all[slot, 2 * k] = block[0:16]
        o_all[slot, 2 * k + 1] = block[16:32]
    own = o_all.at[slot]
    for d in range(1, 4):
        send(own, own, x_send.at[0], x_recv.at[d], (me, pb_peers[2 * d]))
    send(own, own, x_send.at[0], x_recv.at[0], (me, partner))

    values_copy.wait()

    wait_bytes(g_all.at[pl.ds(0, PSG - 1)], recv_sem.at[3])
    ones = jnp.ones((8, 256), BF16)
    for g in range(GROUPS):
        four = pl.ds(g * 4, 4)
        blocks = head_blocks(columns(g_all[four]))
        out_rows = columns(o_all[slot, four]).astype(F32)
        product = blocks.astype(F32) * jnp.concatenate([out_rows] * 4, axis=0)
        delta = sum(dot(ones, part, NT) for part in split_bf16(product, 2))[0:1]
        prob_grad = dot(values[:, g * 256 : (g + 1) * 256], blocks, NT)
        sgrad[g] = (probs[g] * (prob_grad - delta)).astype(BF16)
    row = lax.broadcasted_iota(jnp.int32, (128, 256), 0) // 32
    col = lax.broadcasted_iota(jnp.int32, (128, 256), 1) // 64
    for g in range(GROUPS):
        part = jnp.where(row == col, dot(sgrad[g], keys[:, g * 256 : (g + 1) * 256], TN), 0.0)
        part = (part[0:32] + part[32:64] + part[64:96] + part[96:128]).astype(BF16)
        qpart[g * 4] = part[0:16, 0:128]
        qpart[g * 4 + 1] = part[16:32, 0:128]
        qpart[g * 4 + 2] = part[0:16, 128:256]
        qpart[g * 4 + 3] = part[16:32, 128:256]
    for to in far_first:
        send(qpart.at[to], qpart_in.at[me], send_sem.at[4], recv_sem.at[4], (to, pb))
    qpart_in[me] = qpart[me]

    for g in range(GROUPS):
        wide, four = pl.ds(g * 256, 256), pl.ds(g * 4, 4)
        vgrad[:, wide] = dot(probs_low[g], head_blocks(columns(g_all[four])), NN).astype(BF16)
    vgrad_copy = pltpu.make_async_copy(vgrad, vgrad_out, out_sem.at[0])
    vgrad_copy.start()
    kgrad_copy = pltpu.make_async_copy(sgrad, kgrad_out, out_sem.at[1])
    kgrad_copy.start()
    q_copy = pltpu.make_async_copy(q_all, q_out, out_sem.at[5])
    q_copy.start()

    for d in (1, 3, 2):
        wait_bytes(own, x_recv.at[d])
        got = o_all.at[core * 4 + lax.rem(xpos + 4 - d, 4)]
        send(got, got, x_send.at[0], x_recv.at[0], (me, partner))
    wait_bytes(dg_all.at[pl.ds(0, PB - 1)], x_recv.at[4])
    dg_copy = pltpu.make_async_copy(dg_all, dg_out, out_sem.at[2])
    dg_copy.start()

    wait_bytes(qpart_in.at[pl.ds(0, PSG - 1)], recv_sem.at[4])
    qg_own[...] = jnp.sum(qpart_in[...].astype(F32), axis=0).astype(BF16)
    opposite = core * 4 + lax.rem(xpos + 2, 4)
    send(qg_own, qg_all.at[slot, me], side_send.at[0], side_recv.at[0], (me, pb_peers[4]))
    for to in far_first:
        send(qg_own, qg_all.at[slot, me], send_sem.at[5], recv_sem.at[6 + half_of], (to, pb))
    qg_all[slot, me] = qg_own[...]
    wait_bytes(qg_own, side_recv.at[0])
    for to in far_first:
        send(qg_all.at[opposite, me], qg_all.at[opposite, me], send_sem.at[6], recv_sem.at[8], (to, pb))

    wait_bytes(o_all.at[pl.ds(0, 4)], x_recv.at[0])
    tokens = jnp.concatenate([dg_all[s, 1] for s in range(PB)], axis=0)
    for g in range(GROUPS):
        rows = jnp.concatenate([columns(o_all[s, pl.ds(g * 4, 4)]) for s in range(PB)], axis=0)
        owg[g * 256 : (g + 1) * 256, :] = dot(rows, tokens, TN)
    owg_copy = pltpu.make_async_copy(owg, owg_out, out_sem.at[3])
    owg_copy.start()
    for i, count, ref in (
        (0, PSG - 1, partial), (1, PSG - 1, qa.at[0]), (2, Y - 1, stats), (8, Y - 1, qa.at[1]), (9, PSG - Y, qa.at[1]), (3, PSG - 1, g_all), (4, PSG - 1, qpart),
        (5, PSG - 1, qpart), (7, PSG - Y, stats),
    ):
        wait_bytes(ref.at[pl.ds(0, count)], send_sem.at[i])
    wait_bytes(o_all.at[pl.ds(0, 7)], x_send.at[0])
    wait_bytes(dg_all.at[pl.ds(0, PB - 1)], x_send.at[1])
    wait_bytes(qg_own, side_send.at[0])
    for copy in (vgrad_copy, kgrad_copy, dg_copy, owg_copy, q_copy):
        copy.wait()

    def keep(at, first=0, count=PSG):
        part = pl.ds(first, count)
        pltpu.make_async_copy(qg_all.at[at, part], qg_out.at[at, part], out_sem.at[5]).start()

    def hand_over(at, first, count):
        part = pl.ds(first, count)
        send(qg_all.at[at, part], qg_out.at[at, part], core_send.at[0], core_recv.at[0], (me, partner))

    firsts = (16 * half_of, 16 - 16 * half_of)
    for half, first in enumerate(firsts):
        wait_bytes(qg_all.at[slot, pl.ds(0, 15 + half)], recv_sem.at[6 + half_of if half == 0 else 7 - half_of])
        span = pl.ds(first, 16)
        part = qg_all.at[slot, span]
        if half == 0:
            for d in (2, 6):
                send(part, part, side_send.at[1], side_recv.at[1], (me, pb_peers[d]))
        else:
            for d in (2, 6):
                for to in (pb_peers[d], lax.rem(partner + d, PB)):
                    send(part, qg_out.at[slot, span], side_send.at[1], side_recv.at[2], (me, to))
    hand_over(slot, 0, PSG)
    keep(slot)
    wait_bytes(qg_all.at[slot, pl.ds(0, PSG - 1)], recv_sem.at[8])
    hand_over(opposite, 0, PSG)
    keep(opposite)
    sides = [core * 4 + lax.rem(xpos + d, 4) for d in (3, 1)]
    wait_bytes(qg_all.at[slot], side_recv.at[1])
    for at in sides:
        hand_over(at, firsts[0], 16)
    for at in sides:
        keep(at, firsts[0], 16)
    wait_bytes(qpart.at[pl.ds(0, PSG - 1)], send_sem.at[6])
    wait_bytes(qg_all.at[pl.ds(0, 3)], side_send.at[1])
    wait_bytes(qg_all.at[pl.ds(0, 3)], core_send.at[0])
    wait_bytes(qg_all.at[pl.ds(0, 3)], out_sem.at[5])
    wait_bytes(qg_all.at[pl.ds(0, 2)], side_recv.at[2])
    wait_bytes(qg_all.at[pl.ds(0, 3)], core_recv.at[0])


def grads_kernel(
    kgrad_in, vgrad_in, owg_in, qg_hbm, dg_hbm, qw_hbm, q_hbm, hidden_hbm, kgrad_out, vgrad_out, qwg_hbm, owg_out,
    sgrad, kgrad, vgrad, owg, qg, dg, qw, q_all, hidden, qwg, in_sem, out_sem,
):
    pb = lax.axis_index("pb")
    slot = (pb % 2) * 4 + pb // 2
    loads = []

    def load(src, dst):
        loads.append(pltpu.make_async_copy(src, dst, in_sem.at[len(loads)]))
        loads[-1].start()
        return loads[-1]

    def store(i, src, dst):
        pltpu.make_async_copy(src, dst, out_sem.at[i]).start()

    q_load = load(q_hbm, q_all)
    k_loads = [load(kgrad_in.at[pl.ds(g, 2)], sgrad.at[pl.ds(g, 2)]) for g in range(0, GROUPS, 2)]
    v_loads = [load(vgrad_in.at[pl.ds(i * 256, 256)], vgrad.at[pl.ds(i * 256, 256)]) for i in range(2)]
    dg_load = load(dg_hbm, dg)
    qg_load = load(qg_hbm, qg)
    qw_load = load(qw_hbm, qw)
    owg_load = load(owg_in, owg)

    q_load.wait()
    for g in range(GROUPS):
        if g % 2 == 0:
            k_loads[g // 2].wait()
        wide, four = pl.ds(g * 256, 256), pl.ds(g * 4, 4)
        kgrad[:, wide] = dot(sgrad[g], head_blocks(columns(q_all[four])), NN).astype(BF16)
        if g % 2 == 1:
            both = pl.ds((g - 1) * 256, 512)
            store(1, kgrad.at[:, both], kgrad_out.at[:, both])
    for i in range(2):
        rows = pl.ds(i * 256, 256)
        v_loads[i].wait()
        store(0, vgrad.at[rows], vgrad_out.at[rows])
    dg_load.wait()
    qg_load.wait()
    tokens = jnp.concatenate([dg[s, 0] for s in range(PB)], axis=0)
    for g in range(GROUPS):
        wide, four = pl.ds(g * 256, 256), pl.ds(g * 4, 4)
        qwg[:, wide] = dot(tokens, jnp.concatenate([columns(qg[s, four]) for s in range(PB)], axis=0), TN)
        if g % 4 == 3:
            half = pl.ds((g - 3) * 256, 1024)
            store(2, qwg.at[:, half], qwg_hbm.at[:, half])
    owg_load.wait()
    store(3, owg, owg_out)
    qw_load.wait()
    hidden[...] = sum(
        dot(columns(qg[slot, pl.ds(g * 4, 4)]), qw[:, g * 256 : (g + 1) * 256], NT) for g in range(GROUPS)
    ).astype(BF16)
    store(4, hidden, hidden_hbm)
    for i, ref in enumerate((vgrad, kgrad, qwg, owg, hidden)):
        pltpu.make_async_copy(ref, ref, out_sem.at[i]).wait()


def local(
    dec_hidden, out_grad, query_weight, output_weight, queries, attn_out, row_max, row_sum, keys, values, lengths
):
    hbm = pl.BlockSpec(memory_space=pl.ANY)
    sds = jax.ShapeDtypeStruct
    pieces = (PSG, 16, 128)
    kgrad, vgrad, owg, qg_all, dg_all, q_all = pl.pallas_call(
        comm_kernel,
        out_shape=[
            sds((GROUPS, 512, 128), BF16), sds((512, 2048), BF16), sds((2048, 128), F32),
            sds((PB,) + pieces, BF16), sds((PB, 2, 32, 128), BF16), sds(pieces, BF16),
        ],
        in_specs=[hbm] * 10,
        out_specs=[hbm] * 6,
        scratch_shapes=[
            pltpu.VMEM((2048, 128), BF16),
            pltpu.VMEM((512, 2048), BF16),
            pltpu.VMEM((512, 2048), BF16),
            pltpu.VMEM((1, 2048), BF16),
            pltpu.VMEM((1, 2048), BF16),
            pltpu.VMEM((1, 32), F32),
            pltpu.VMEM((1, 32), F32),
            pltpu.SMEM((1, 2), jnp.int32),
            pltpu.VMEM((32, 128), F32),
            pltpu.VMEM((2, PSG, 16, 128), BF16),
            pltpu.VMEM((PSG, 16, 128), F32),
            pltpu.VMEM((1, 128), F32),
            pltpu.VMEM((PSG, 1, 128), F32),
            pltpu.VMEM(pieces, BF16),
            pltpu.VMEM(pieces, BF16),
            pltpu.VMEM((16, 128), BF16),
            pltpu.VMEM(pieces, BF16),
            pltpu.VMEM(pieces, BF16),
            pltpu.VMEM((GROUPS, 512, 128), F32),
            pltpu.VMEM((GROUPS, 512, 128), BF16),
            pltpu.VMEM((GROUPS, 512, 128), BF16),
            pltpu.VMEM((512, 2048), BF16),
            pltpu.VMEM((2048, 128), F32),
            pltpu.VMEM(pieces, BF16),
            pltpu.VMEM(pieces, BF16),
            pltpu.VMEM((16, 128), BF16),
            pltpu.VMEM((PB,) + pieces, BF16),
            pltpu.VMEM((PB,) + pieces, BF16),
            pltpu.VMEM((2, 32, 128), BF16),
            pltpu.VMEM((PB, 2, 32, 128), BF16),
            pltpu.SemaphoreType.DMA((10,)),
            pltpu.SemaphoreType.DMA((10,)),
            pltpu.SemaphoreType.DMA((11,)),
            pltpu.SemaphoreType.DMA((2,)),
            pltpu.SemaphoreType.DMA((5,)),
            pltpu.SemaphoreType.DMA((2,)),
            pltpu.SemaphoreType.DMA((3,)),
            pltpu.SemaphoreType.DMA((1,)),
            pltpu.SemaphoreType.DMA((1,)),
            pltpu.SemaphoreType.DMA((6,)),
        ],
        compiler_params=pltpu.CompilerParams(collective_id=1, has_side_effects=True, vmem_limit_bytes=62 * 2**20),
        cost_estimate=pl.CostEstimate(flops=10**9, bytes_accessed=10**7, transcendentals=512 * 1024),
        name="comm",
    )(
        dec_hidden.reshape(32, 128), out_grad.reshape(32, 128), output_weight,
        queries.reshape(1, 2048), attn_out.reshape(1, 2048), row_max.reshape(1, 32), row_sum.reshape(1, 32),
        keys.reshape(512, 2048), values.reshape(512, 2048), lengths,
    )

    hidden, kgrad, vgrad, qwg, owg = pl.pallas_call(
        grads_kernel,
        out_shape=[
            sds((32, 128), BF16), sds((512, 2048), BF16), sds((512, 2048), BF16),
            sds((128, 2048), F32), sds((2048, 128), F32),
        ],
        in_specs=[hbm] * 7,
        out_specs=[hbm] * 5,
        scratch_shapes=[
            pltpu.VMEM((GROUPS, 512, 128), BF16),
            pltpu.VMEM((512, 2048), BF16),
            pltpu.VMEM((512, 2048), BF16),
            pltpu.VMEM((2048, 128), F32),
            pltpu.VMEM((PB,) + pieces, BF16),
            pltpu.VMEM((PB, 2, 32, 128), BF16),
            pltpu.VMEM((128, 2048), BF16),
            pltpu.VMEM(pieces, BF16),
            pltpu.VMEM((32, 128), BF16),
            pltpu.VMEM((128, 2048), F32),
            pltpu.SemaphoreType.DMA((14,)),
            pltpu.SemaphoreType.DMA((5,)),
        ],
        compiler_params=pltpu.CompilerParams(vmem_limit_bytes=62 * 2**20),
        cost_estimate=pl.CostEstimate(flops=10**9, bytes_accessed=10**7, transcendentals=0),
        name="grads",
    )(kgrad, vgrad, owg, qg_all, dg_all, query_weight, q_all)
    return (
        hidden.reshape(dec_hidden.shape), kgrad.reshape(keys.shape), vgrad.reshape(values.shape), qwg, owg
    )


def solution(mesh):
    in_specs = (
        P("pb", None, "psg"),
        P("pb", None, "psg"),
        P("psg", None),
        P(None, "psg"),
        P("pb", "psg", None),
        P("pb", "psg", None),
        P("pb", "psg", None),
        P("pb", "psg", None),
        P("pb", "psg", None, None),
        P("pb", "psg", None, None),
        P("pb", "psg"),
    )
    out_specs = (
        P("pb", None, "psg"),
        P("pb", "psg", None, None),
        P("pb", "psg", None, None),
        P("psg", None),
        P(None, "psg"),
    )
    return jax.shard_map(local, mesh=mesh, in_specs=in_specs, out_specs=out_specs, check_vma=False)
```

```python
import jax
import jax.numpy as jnp
from jax import lax
from jax.experimental import pallas as pl
from jax.experimental.pallas import tpu as pltpu
from jax.sharding import PartitionSpec as P

MESH = pl.DeviceIdType.MESH
F32 = jnp.float32
BF16 = jnp.bfloat16

NT = (((1,), (1,)), ((), ()))
TN = (((0,), (0,)), ((), ()))
NN = (((1,), (0,)), ((), ()))

Z, Y, PSG, PB = 8, 4, 32, 8
GROUPS = 8
NEAR = (0, 1, 7, 2, 6, 3, 5, 4)


def dot(a, b, dims):
    return lax.dot_general(a, b, dims, preferred_element_type=F32)


def columns(pieces):
    left = jnp.concatenate([pieces[0], pieces[1]], axis=0)
    right = jnp.concatenate([pieces[2], pieces[3]], axis=0)
    return jnp.concatenate([left, right], axis=1)


def head_blocks(rows):
    tiled = jnp.concatenate([rows] * 4, axis=0)
    row = lax.broadcasted_iota(jnp.int32, tiled.shape, 0) // 32
    col = lax.broadcasted_iota(jnp.int32, tiled.shape, 1) // 64
    return jnp.where(row == col, tiled, jnp.zeros_like(tiled))


def split_bf16(x, terms):
    out = []
    for _ in range(terms):
        part = x.astype(BF16)
        out.append(part)
        x = x - part.astype(F32)
    return out


def comm_kernel(
    dec_hbm, grad_hbm, weight_hbm, query_hbm, attn_hbm, max_hbm, sum_hbm, keys_hbm, values_hbm, len_hbm,
    kgrad_out, vgrad_out, owg_out, qg_out, dg_out, q_out,
    weight, keys, values, query_ref, attn_ref, max_ref, sum_ref, len_ref, bundle, qa, qa32, stat_src, stats,
    partial, part_in, g_own, g_all, q_all, probs, probs_low, sgrad, vgrad, owg, qpart, qpart_in, qg_own, qg_all,
    o_all, dg_src, dg_all,
    local_sem, send_sem, recv_sem, x_send, x_recv, side_send, side_recv, core_send,
    core_recv, out_sem,
):
    me, pb = lax.axis_index("psg"), lax.axis_index("pb")
    z, y = lax.div(me, Y), lax.rem(me, Y)
    half_of = lax.div(z, 4)
    core, xpos = lax.rem(pb, 2), lax.div(pb, 2)
    slot = core * 4 + xpos
    partner = pb + 1 - 2 * core
    zs = [lax.rem(z + d, Z) for d in range(Z)]
    ys = [lax.rem(y + d, Y) for d in range(Y)]
    peers = {(dz, dy): zs[dz] * Y + ys[dy] for dz in range(Z) for dy in range(Y) if dz or dy}
    far_first = [peers[dz, dy] for dz in reversed(NEAR) for dy in (2, 1, 3, 0) if dz or dy]
    pb_peers = [lax.rem(pb + d, PB) for d in range(PB)]

    barrier = pltpu.get_barrier_semaphore()
    for to in far_first:
        pl.semaphore_signal(barrier, inc=1, device_id=(to, pb), device_id_type=MESH)
    for d in range(1, PB):
        pl.semaphore_signal(barrier, inc=1, device_id=(me, pb_peers[d]), device_id_type=MESH)

    loads = [
        pltpu.make_async_copy(src, dst, local_sem.at[i])
        for i, (src, dst) in enumerate((
            (query_hbm, query_ref), (attn_hbm, attn_ref), (max_hbm, max_ref), (sum_hbm, sum_ref),
            (dec_hbm, dg_src.at[0]), (grad_hbm, dg_src.at[1]), (weight_hbm, weight), (len_hbm, len_ref),
            (keys_hbm, keys), (values_hbm, values),
        ))
    ]
    for load in loads:
        load.start()
    keys_copy, values_copy = loads[8:]
    for load in loads[:6]:
        load.wait()

    for k in range(16):
        bundle[k : k + 1, :] = query_ref[:, k * 128 : (k + 1) * 128].astype(F32)
        bundle[16 + k : 17 + k, :] = attn_ref[:, k * 128 : (k + 1) * 128].astype(F32)
    qa[0, me] = bundle[0:16].astype(BF16)
    qa[1, me] = bundle[16:32].astype(BF16)
    stat_src[...] = jnp.zeros_like(stat_src)
    stat_src[0:1, 0:32] = max_ref[...] + jnp.log(sum_ref[...])
    stats[me] = stat_src[...]
    dg_all[slot] = dg_src[...]

    loads[6].wait()
    loads[7].wait()
    grad = dg_src[1]
    for k in range(16):
        block = dot(grad, weight[k * 128 : (k + 1) * 128, :], NT).astype(BF16)
        partial[2 * k] = block[0:16]
        partial[2 * k + 1] = block[16:32]

    pl.semaphore_wait(barrier, PSG - 1 + PB - 1)

    def send(src, dst, send_at, recv_at, to):
        pltpu.make_async_remote_copy(
            src_ref=src, dst_ref=dst, send_sem=send_at, recv_sem=recv_at, device_id=to, device_id_type=MESH
        ).start()

    def wait_bytes(ref, sem):
        pltpu.make_async_copy(ref, ref, sem).wait()

    for to in far_first:
        send(partial.at[to], part_in.at[me], send_sem.at[0], recv_sem.at[0], (to, pb))
    part_in[me] = partial[me]
    for dy in (2, 1, 3):
        send(qa.at[1, me], qa.at[1, me], send_sem.at[8], recv_sem.at[9], (peers[0, dy], pb))
        send(stats.at[me], stats.at[me], send_sem.at[2], recv_sem.at[2], (peers[0, dy], pb))
    for to in far_first:
        send(qa.at[0, me], qa.at[0, me], send_sem.at[1], recv_sem.at[1], (to, pb))
    row_of_four = pl.ds(z * Y, Y)
    wait_bytes(stats.at[pl.ds(0, Y - 1)], recv_sem.at[2])
    for dz in (4, 5, 3, 6, 2, 7, 1):
        send(stats.at[row_of_four], stats.at[row_of_four], send_sem.at[7], recv_sem.at[5], (peers[dz, 0], pb))

    wait_bytes(part_in.at[pl.ds(0, PSG - 1)], recv_sem.at[0])
    g_own[...] = jnp.sum(part_in[...].astype(F32), axis=0).astype(BF16)
    for to in far_first:
        send(g_own, g_all.at[me], send_sem.at[3], recv_sem.at[3], (to, pb))
    g_all[me] = g_own[...]
    wait_bytes(qa.at[1, pl.ds(0, Y - 1)], recv_sem.at[9])
    for dz in (4, 5, 3, 6, 2, 7, 1):
        rows = qa.at[1, row_of_four]
        send(rows, rows, send_sem.at[9], recv_sem.at[10], (peers[dz, 0], pb))
    for d in range(1, PB):
        send(dg_src, dg_all.at[slot], x_send.at[1], x_recv.at[4], (me, pb_peers[d]))

    wait_bytes(qa.at[0, pl.ds(0, PSG - 1)], recv_sem.at[1])
    qa32[...] = qa[0].astype(F32)
    for k in range(16):
        block = qa32[:, k, :].astype(BF16)
        q_all[2 * k] = block[0:16]
        q_all[2 * k + 1] = block[16:32]

    wait_bytes(stats.at[pl.ds(0, PSG - Y)], recv_sem.at[5])
    stat_rows = jnp.concatenate([stats[t] for t in range(PSG)], axis=0)
    head = lax.broadcasted_iota(jnp.int32, (128, 1024), 0)
    lane = lax.broadcasted_iota(jnp.int32, (128, 1024), 1)
    pick = jnp.where(head == lane // 32, 1.0, 0.0).astype(BF16)
    spread = sum(dot(part, pick, NN) for part in split_bf16(stat_rows, 3))
    token = lax.broadcasted_iota(jnp.int32, (32, 1024), 0)
    lane = lax.broadcasted_iota(jnp.int32, (32, 1024), 1)
    stat_lanes = jnp.sum(jnp.where(token == lane % 32, spread, 0.0), axis=0, keepdims=True)

    keys_copy.wait()
    position = lax.broadcasted_iota(jnp.int32, (256, 128), 0)
    for g in range(GROUPS):
        blocks = head_blocks(columns(q_all[pl.ds(g * 4, 4)]))
        scores = dot(keys[:, g * 256 : (g + 1) * 256], blocks, NT) - stat_lanes[:, g * 128 : (g + 1) * 128]
        for p in range(2):
            rows = pl.ds(p * 256, 256)
            value = jnp.where(position < len_ref[0, p], jnp.exp(scores[p * 256 : (p + 1) * 256]), 0.0)
            probs[g, rows] = value
            probs_low[g, rows] = value.astype(BF16)
    wait_bytes(qa.at[1, pl.ds(0, PSG - Y)], recv_sem.at[10])
    qa32[...] = qa[1].astype(F32)
    for k in range(16):
        block = qa32[:, k, :].astype(BF16)
        o_all[slot, 2 * k] = block[0:16]
        o_all[slot, 2 * k + 1] = block[16:32]
    own = o_all.at[slot]
    for d in range(1, 4):
        send(own, own, x_send.at[0], x_recv.at[d], (me, pb_peers[2 * d]))
    send(own, own, x_send.at[0], x_recv.at[0], (me, partner))

    values_copy.wait()

    wait_bytes(g_all.at[pl.ds(0, PSG - 1)], recv_sem.at[3])
    ones = jnp.ones((8, 256), BF16)
    for g in range(GROUPS):
        four = pl.ds(g * 4, 4)
        blocks = head_blocks(columns(g_all[four]))
        out_rows = columns(o_all[slot, four]).astype(F32)
        product = blocks.astype(F32) * jnp.concatenate([out_rows] * 4, axis=0)
        delta = sum(dot(ones, part, NT) for part in split_bf16(product, 2))[0:1]
        prob_grad = dot(values[:, g * 256 : (g + 1) * 256], blocks, NT)
        sgrad[g] = (probs[g] * (prob_grad - delta)).astype(BF16)
    row = lax.broadcasted_iota(jnp.int32, (128, 256), 0) // 32
    col = lax.broadcasted_iota(jnp.int32, (128, 256), 1) // 64
    for g in range(GROUPS):
        part = jnp.where(row == col, dot(sgrad[g], keys[:, g * 256 : (g + 1) * 256], TN), 0.0)
        part = (part[0:32] + part[32:64] + part[64:96] + part[96:128]).astype(BF16)
        qpart[g * 4] = part[0:16, 0:128]
        qpart[g * 4 + 1] = part[16:32, 0:128]
        qpart[g * 4 + 2] = part[0:16, 128:256]
        qpart[g * 4 + 3] = part[16:32, 128:256]
    for to in far_first:
        send(qpart.at[to], qpart_in.at[me], send_sem.at[4], recv_sem.at[4], (to, pb))
    qpart_in[me] = qpart[me]

    for g in range(GROUPS):
        wide, four = pl.ds(g * 256, 256), pl.ds(g * 4, 4)
        vgrad[:, wide] = dot(probs_low[g], head_blocks(columns(g_all[four])), NN).astype(BF16)
    vgrad_copy = pltpu.make_async_copy(vgrad, vgrad_out, out_sem.at[0])
    vgrad_copy.start()
    kgrad_copy = pltpu.make_async_copy(sgrad, kgrad_out, out_sem.at[1])
    kgrad_copy.start()
    q_copy = pltpu.make_async_copy(q_all, q_out, out_sem.at[5])
    q_copy.start()

    for d in (1, 3, 2):
        wait_bytes(own, x_recv.at[d])
        got = o_all.at[core * 4 + lax.rem(xpos + 4 - d, 4)]
        send(got, got, x_send.at[0], x_recv.at[0], (me, partner))
    wait_bytes(dg_all.at[pl.ds(0, PB - 1)], x_recv.at[4])
    dg_copy = pltpu.make_async_copy(dg_all, dg_out, out_sem.at[2])
    dg_copy.start()

    wait_bytes(qpart_in.at[pl.ds(0, PSG - 1)], recv_sem.at[4])
    qg_own[...] = jnp.sum(qpart_in[...].astype(F32), axis=0).astype(BF16)
    opposite = core * 4 + lax.rem(xpos + 2, 4)
    send(qg_own, qg_all.at[slot, me], side_send.at[0], side_recv.at[0], (me, pb_peers[4]))
    for to in far_first:
        send(qg_own, qg_all.at[slot, me], send_sem.at[5], recv_sem.at[6 + half_of], (to, pb))
    qg_all[slot, me] = qg_own[...]
    wait_bytes(qg_own, side_recv.at[0])
    for to in far_first:
        send(qg_all.at[opposite, me], qg_all.at[opposite, me], send_sem.at[6], recv_sem.at[8], (to, pb))

    def keep(at, first=0, count=PSG):
        part = pl.ds(first, count)
        pltpu.make_async_copy(qg_all.at[at, part], qg_out.at[at, part], out_sem.at[5]).start()

    def hand_over(at, first, count):
        part = pl.ds(first, count)
        send(qg_all.at[at, part], qg_out.at[at, part], core_send.at[0], core_recv.at[0], (me, partner))

    firsts = (16 * half_of, 16 - 16 * half_of)
    for half, first in enumerate(firsts):
        wait_bytes(qg_all.at[slot, pl.ds(0, 15 + half)], recv_sem.at[6 + half_of if half == 0 else 7 - half_of])
        span = pl.ds(first, 16)
        part = qg_all.at[slot, span]
        if half == 0:
            for d in (2, 6):
                send(part, part, side_send.at[1], side_recv.at[1], (me, pb_peers[d]))
        else:
            for d in (2, 6):
                for to in (pb_peers[d], lax.rem(partner + d, PB)):
                    send(part, qg_out.at[slot, span], side_send.at[1], side_recv.at[2], (me, to))
    hand_over(slot, 0, PSG)
    keep(slot)

    wait_bytes(o_all.at[pl.ds(0, 4)], x_recv.at[0])
    tokens = jnp.concatenate([dg_all[s, 1] for s in range(PB)], axis=0)
    for g in range(GROUPS):
        rows = jnp.concatenate([columns(o_all[s, pl.ds(g * 4, 4)]) for s in range(PB)], axis=0)
        owg[g * 256 : (g + 1) * 256, :] = dot(rows, tokens, TN)
    owg_copy = pltpu.make_async_copy(owg, owg_out, out_sem.at[3])
    owg_copy.start()

    for i, count, ref in (
        (0, PSG - 1, partial), (1, PSG - 1, qa.at[0]), (2, Y - 1, stats), (8, Y - 1, qa.at[1]), (9, PSG - Y, qa.at[1]), (3, PSG - 1, g_all), (4, PSG - 1, qpart),
        (5, PSG - 1, qpart), (7, PSG - Y, stats),
    ):
        wait_bytes(ref.at[pl.ds(0, count)], send_sem.at[i])
    wait_bytes(o_all.at[pl.ds(0, 7)], x_send.at[0])
    wait_bytes(dg_all.at[pl.ds(0, PB - 1)], x_send.at[1])
    wait_bytes(qg_own, side_send.at[0])
    for copy in (vgrad_copy, kgrad_copy, dg_copy, q_copy):
        copy.wait()

    sides = [core * 4 + lax.rem(xpos + d, 4) for d in (3, 1)]
    wait_bytes(qg_all.at[slot], side_recv.at[1])
    for at in sides:
        hand_over(at, firsts[0], 16)
    for at in sides:
        keep(at, firsts[0], 16)
    wait_bytes(qg_all.at[slot, pl.ds(0, PSG - 1)], recv_sem.at[8])
    hand_over(opposite, 0, PSG)
    keep(opposite)
    wait_bytes(qpart.at[pl.ds(0, PSG - 1)], send_sem.at[6])
    wait_bytes(qg_all.at[pl.ds(0, 3)], side_send.at[1])
    wait_bytes(qg_all.at[pl.ds(0, 3)], core_send.at[0])
    wait_bytes(qg_all.at[pl.ds(0, 3)], out_sem.at[5])
    wait_bytes(qg_all.at[pl.ds(0, 2)], side_recv.at[2])
    wait_bytes(qg_all.at[pl.ds(0, 3)], core_recv.at[0])
    owg_copy.wait()


def grads_kernel(
    kgrad_in, vgrad_in, owg_in, qg_hbm, dg_hbm, qw_hbm, q_hbm, hidden_hbm, kgrad_out, vgrad_out, qwg_hbm, owg_out,
    sgrad, kgrad, vgrad, owg, qg, dg, qw, q_all, hidden, qwg, in_sem, out_sem,
):
    pb = lax.axis_index("pb")
    slot = (pb % 2) * 4 + pb // 2
    loads = []

    def load(src, dst):
        loads.append(pltpu.make_async_copy(src, dst, in_sem.at[len(loads)]))
        loads[-1].start()
        return loads[-1]

    def store(i, src, dst):
        pltpu.make_async_copy(src, dst, out_sem.at[i]).start()

    q_load = load(q_hbm, q_all)
    k_loads = [load(kgrad_in.at[pl.ds(g, 2)], sgrad.at[pl.ds(g, 2)]) for g in range(0, GROUPS, 2)]
    v_loads = [load(vgrad_in.at[pl.ds(i * 256, 256)], vgrad.at[pl.ds(i * 256, 256)]) for i in range(2)]
    dg_load = load(dg_hbm, dg)
    qg_load = load(qg_hbm, qg)
    qw_load = load(qw_hbm, qw)
    owg_load = load(owg_in, owg)

    q_load.wait()
    for g in range(GROUPS):
        if g % 2 == 0:
            k_loads[g // 2].wait()
        wide, four = pl.ds(g * 256, 256), pl.ds(g * 4, 4)
        kgrad[:, wide] = dot(sgrad[g], head_blocks(columns(q_all[four])), NN).astype(BF16)
        if g % 2 == 1:
            both = pl.ds((g - 1) * 256, 512)
            store(1, kgrad.at[:, both], kgrad_out.at[:, both])
    for i in range(2):
        rows = pl.ds(i * 256, 256)
        v_loads[i].wait()
        store(0, vgrad.at[rows], vgrad_out.at[rows])
    dg_load.wait()
    qg_load.wait()
    tokens = jnp.concatenate([dg[s, 0] for s in range(PB)], axis=0)
    for g in range(GROUPS):
        wide, four = pl.ds(g * 256, 256), pl.ds(g * 4, 4)
        qwg[:, wide] = dot(tokens, jnp.concatenate([columns(qg[s, four]) for s in range(PB)], axis=0), TN)
        if g % 4 == 3:
            half = pl.ds((g - 3) * 256, 1024)
            store(2, qwg.at[:, half], qwg_hbm.at[:, half])
    owg_load.wait()
    store(3, owg, owg_out)
    qw_load.wait()
    hidden[...] = sum(
        dot(columns(qg[slot, pl.ds(g * 4, 4)]), qw[:, g * 256 : (g + 1) * 256], NT) for g in range(GROUPS)
    ).astype(BF16)
    store(4, hidden, hidden_hbm)
    for i, ref in enumerate((vgrad, kgrad, qwg, owg, hidden)):
        pltpu.make_async_copy(ref, ref, out_sem.at[i]).wait()


def local(
    dec_hidden, out_grad, query_weight, output_weight, queries, attn_out, row_max, row_sum, keys, values, lengths
):
    hbm = pl.BlockSpec(memory_space=pl.ANY)
    sds = jax.ShapeDtypeStruct
    pieces = (PSG, 16, 128)
    kgrad, vgrad, owg, qg_all, dg_all, q_all = pl.pallas_call(
        comm_kernel,
        out_shape=[
            sds((GROUPS, 512, 128), BF16), sds((512, 2048), BF16), sds((2048, 128), F32),
            sds((PB,) + pieces, BF16), sds((PB, 2, 32, 128), BF16), sds(pieces, BF16),
        ],
        in_specs=[hbm] * 10,
        out_specs=[hbm] * 6,
        scratch_shapes=[
            pltpu.VMEM((2048, 128), BF16),
            pltpu.VMEM((512, 2048), BF16),
            pltpu.VMEM((512, 2048), BF16),
            pltpu.VMEM((1, 2048), BF16),
            pltpu.VMEM((1, 2048), BF16),
            pltpu.VMEM((1, 32), F32),
            pltpu.VMEM((1, 32), F32),
            pltpu.SMEM((1, 2), jnp.int32),
            pltpu.VMEM((32, 128), F32),
            pltpu.VMEM((2, PSG, 16, 128), BF16),
            pltpu.VMEM((PSG, 16, 128), F32),
            pltpu.VMEM((1, 128), F32),
            pltpu.VMEM((PSG, 1, 128), F32),
            pltpu.VMEM(pieces, BF16),
            pltpu.VMEM(pieces, BF16),
            pltpu.VMEM((16, 128), BF16),
            pltpu.VMEM(pieces, BF16),
            pltpu.VMEM(pieces, BF16),
            pltpu.VMEM((GROUPS, 512, 128), F32),
            pltpu.VMEM((GROUPS, 512, 128), BF16),
            pltpu.VMEM((GROUPS, 512, 128), BF16),
            pltpu.VMEM((512, 2048), BF16),
            pltpu.VMEM((2048, 128), F32),
            pltpu.VMEM(pieces, BF16),
            pltpu.VMEM(pieces, BF16),
            pltpu.VMEM((16, 128), BF16),
            pltpu.VMEM((PB,) + pieces, BF16),
            pltpu.VMEM((PB,) + pieces, BF16),
            pltpu.VMEM((2, 32, 128), BF16),
            pltpu.VMEM((PB, 2, 32, 128), BF16),
            pltpu.SemaphoreType.DMA((10,)),
            pltpu.SemaphoreType.DMA((10,)),
            pltpu.SemaphoreType.DMA((11,)),
            pltpu.SemaphoreType.DMA((2,)),
            pltpu.SemaphoreType.DMA((5,)),
            pltpu.SemaphoreType.DMA((2,)),
            pltpu.SemaphoreType.DMA((3,)),
            pltpu.SemaphoreType.DMA((1,)),
            pltpu.SemaphoreType.DMA((1,)),
            pltpu.SemaphoreType.DMA((6,)),
        ],
        compiler_params=pltpu.CompilerParams(collective_id=1, has_side_effects=True, vmem_limit_bytes=62 * 2**20),
        cost_estimate=pl.CostEstimate(flops=10**9, bytes_accessed=10**7, transcendentals=512 * 1024),
        name="comm",
    )(
        dec_hidden.reshape(32, 128), out_grad.reshape(32, 128), output_weight,
        queries.reshape(1, 2048), attn_out.reshape(1, 2048), row_max.reshape(1, 32), row_sum.reshape(1, 32),
        keys.reshape(512, 2048), values.reshape(512, 2048), lengths,
    )

    hidden, kgrad, vgrad, qwg, owg = pl.pallas_call(
        grads_kernel,
        out_shape=[
            sds((32, 128), BF16), sds((512, 2048), BF16), sds((512, 2048), BF16),
            sds((128, 2048), F32), sds((2048, 128), F32),
        ],
        in_specs=[hbm] * 7,
        out_specs=[hbm] * 5,
        scratch_shapes=[
            pltpu.VMEM((GROUPS, 512, 128), BF16),
            pltpu.VMEM((512, 2048), BF16),
            pltpu.VMEM((512, 2048), BF16),
            pltpu.VMEM((2048, 128), F32),
            pltpu.VMEM((PB,) + pieces, BF16),
            pltpu.VMEM((PB, 2, 32, 128), BF16),
            pltpu.VMEM((128, 2048), BF16),
            pltpu.VMEM(pieces, BF16),
            pltpu.VMEM((32, 128), BF16),
            pltpu.VMEM((128, 2048), F32),
            pltpu.SemaphoreType.DMA((14,)),
            pltpu.SemaphoreType.DMA((5,)),
        ],
        compiler_params=pltpu.CompilerParams(vmem_limit_bytes=62 * 2**20),
        cost_estimate=pl.CostEstimate(flops=10**9, bytes_accessed=10**7, transcendentals=0),
        name="grads",
    )(kgrad, vgrad, owg, qg_all, dg_all, query_weight, q_all)
    return (
        hidden.reshape(dec_hidden.shape), kgrad.reshape(keys.shape), vgrad.reshape(values.shape), qwg, owg
    )


def solution(mesh):
    in_specs = (
        P("pb", None, "psg"),
        P("pb", None, "psg"),
        P("psg", None),
        P(None, "psg"),
        P("pb", "psg", None),
        P("pb", "psg", None),
        P("pb", "psg", None),
        P("pb", "psg", None),
        P("pb", "psg", None, None),
        P("pb", "psg", None, None),
        P("pb", "psg"),
    )
    out_specs = (
        P("pb", None, "psg"),
        P("pb", "psg", None, None),
        P("pb", "psg", None, None),
        P("psg", None),
        P(None, "psg"),
    )
    return jax.shard_map(local, mesh=mesh, in_specs=in_specs, out_specs=out_specs, check_vma=False)
```
